32 devices in a mesh: runs: 2 (over x), tile: 16 (over z, y, core).
Axes of the slice: x: 2, y: 2, z: 4, core: 2. Of those that a mesh axis runs over, the one named last changes fastest.
Arguments:
- fluid_press: float32 [8192, 128], P(('runs', 'tile')), parts along dimension 0, may hold values from -6 to 6
- iterate: float32 [8192, 128], P(('runs', 'tile')), parts along dimension 0, may hold values from -6 to 6
- displace: float32 [4096, 128], P(('runs', 'tile')), parts along dimension 0, may hold values from -6 to 6
- velocity: float32 [4096, 128], P(('runs', 'tile')), parts along dimension 0, may hold values from -6 to 6
- stiffness: float32 [4096, 128], P(('runs', 'tile')), parts along dimension 0, may hold values from 0.08 to 0.45
- owners: int32 [4096, 1], P(('runs', 'tile')), parts along dimension 0, may hold values from 0 to 15; in each aligned block of 128 rows (0 to 127, 128 to 255, ...) at most 16 rows name the same one
- diff_cur: bfloat16 [40, 8192, 128], P(None, ('runs', 'tile')), parts along dimension 1, may hold values from -1.1048543 to 1.1048543
- step_cur: bfloat16 [40, 8192, 128], P(None, ('runs', 'tile')), parts along dimension 1, may hold values from -6 to 6
- diff_past: bfloat16 [30, 8192, 128], P(None, ('runs', 'tile')), parts along dimension 1, may hold values from -1.1048543 to 1.1048543
- step_past: bfloat16 [30, 8192, 128], P(None, ('runs', 'tile')), parts along dimension 1, may hold values from -6 to 6
Outputs:
- new_iterate: float32 [8192, 128], P(('runs', 'tile')), parts along dimension 0
- displace_out: float32 [4096, 128], P(('runs', 'tile')), parts along dimension 0
- velocity_out: float32 [4096, 128], P(('runs', 'tile')), parts along dimension 0
The draws below stay inside these ranges and needn't reach their ends.
There are 2 independent parts, one for each index of `runs`. The reference program is written for one: setup_inputs(seed, part) draws one part's arguments, and reference() takes and returns one part's arrays. A program takes and returns all parts, laid end to end along the dimension named above; each array names one. Nothing has to cross between parts.
Inputs may be any that keep to these rules, and one draw needn't show every extreme that they name: `owners`: in the 128 lines of one device no partition is named more than 16 times; some partition is named exactly 16 times.
All inputs are finite; a program needn't handle non-finite values.
Results may differ from the reference program's by a relative error of at most 0.0042.
Values sent between devices are 32-bit elements; how exact they have to be, the bound alone decides.
A program may use at most 64 MiB of HBM per device.

```python
import math
import jax
import jax.numpy as jnp
import numpy as np
from jax import lax

LINE = 128
BLK_DEV = 128
CUR = 40
PAST = 30
SUBSTEPS = 4
MOST = 16
SLOTS_DEV = 256
BLOCKS = 2048
FLUID_ROWS = 4096
N_TILE = 16


def shared_parts(key):
    common = jax.random.truncated_normal(jax.random.fold_in(key, 7), -4.0, 4.0, (FLUID_ROWS, LINE))
    weight = 0.5
    return (common, weight)


def history(key, marker, count):
    common, weight = shared_parts(key)
    own_part = jax.random.truncated_normal(jax.random.fold_in(key, marker), -4.0, 4.0, (count, FLUID_ROWS, LINE))
    col_scale = jnp.exp(jax.random.uniform(jax.random.fold_in(key, marker + 1), (count, 1, 1), minval=0.0, maxval=math.log(10.0)))
    norm = (FLUID_ROWS * LINE) ** (-0.5)
    values = (own_part + weight * common[None]) * col_scale * norm
    return values.astype(jnp.bfloat16)


def draw_diff_cur(key, part):
    return history(key, 11, CUR)


def draw_diff_past(key, part):
    return history(key, 21, PAST)


def level_of(own_key, shape, split, low, top_value):
    def one(position, parts):
        steps = jax.random.uniform(jax.random.fold_in(jax.random.fold_in(own_key, 6), position), (parts,), jnp.float32, low / len(split), top_value / len(split))
        return jnp.repeat(jnp.exp(steps), shape[position] // parts).reshape((-1,) + (1,) * (len(shape) - position - 1))

    level = one(*split[0])
    for cut in split[1:]:
        level = level * one(*cut)
    return level


def assign_block(stream_key, own, number, rows, number_of, top, reach, lean):
    order = jax.random.permutation(stream_key, number_of)
    heavy_load, usual = load_shares(number_of, rows * top, reach, lean, True), load_shares(number_of, rows * top, reach, lean, False)
    places = jnp.arange(number_of)

    def named(sizes, offset_by):
        used = int((sizes > 0).sum())
        fixed = max(1, used // 4)
        passed = fixed + (places - fixed + offset_by * (used - fixed)) % max(1, number_of - fixed)
        return jnp.zeros((number_of,), jnp.int32).at[order[jnp.where(places < fixed, places, passed)]].set(jnp.asarray(sizes, jnp.int32))

    sizes = jnp.where(number % 4 == 0, named(heavy_load, number // 4), named(usual, number - number // 4 - 1))
    mixed = jax.random.permutation(jax.random.fold_in(own, 3), number_of)
    donor, sink = mixed[0:number_of // 2 * 2:2], mixed[1:number_of // 2 * 2:2]
    slack = jnp.minimum(sizes[donor] - 1, reach - sizes[sink]) // 2
    slack = jnp.where((donor == order[0]) | (sink == order[0]) | (sizes[sink] == 0), 0, jnp.maximum(slack, 0))
    passed = jax.random.randint(jax.random.fold_in(own, 4), (number_of // 2,), 0, 1 << 20) % (slack + 1)
    sizes = sizes.at[donor].add(-passed).at[sink].add(passed)
    labels = jnp.searchsorted(jnp.cumsum(sizes), jnp.arange(rows * top), side="right").astype(jnp.int32)
    listing = labels.reshape(top, rows).T
    listing = listing[jax.random.permutation(jax.random.fold_in(own, 1), rows)]
    offset_by = jax.random.randint(jax.random.fold_in(own, 2), (rows, 1), 0, top)
    return jnp.take_along_axis(listing, (jnp.arange(top)[None, :] + offset_by) % top, axis=1)


def load_shares(amount, total, bound, skew, full):
    weights = [(1 << 20) // math.isqrt(standing ** skew) + 1 for standing in range(1, amount + 1)]
    largest = bound if full else min(bound, max(-(-total // amount), total * weights[0] // sum(weights)))
    least = 1 if total - largest >= amount - 1 else 0
    holding, spare = [largest] + [least] * (amount - 1), total - largest - least * (amount - 1)
    while spare > 0:
        free = [i for i in range(1, amount) if holding[i] < largest] or [i for i in range(1, amount) if holding[i] < bound]
        whole, left = sum([weights[i] for i in free]), spare
        for i in free:
            extra = min(bound - holding[i], max(1, left * weights[i] // whole), spare)
            holding[i] = holding[i] + extra
            spare = spare - extra
    return np.array(holding)


def normal_values(stream_key, extent, spread, reach, shards=(), kind=jnp.bfloat16):
    drawn = spread * jax.random.normal(stream_key, extent, jnp.float32)
    if shards:
        drawn = drawn * level_of(stream_key, extent, shards, -0.22, 0.18)
    return jnp.clip(drawn, -reach, reach).astype(kind)


def setup_inputs(seed: int = 0, part: int = 0) -> dict:
    seeds = jax.random.split(jax.random.key(seed), 11)
    part_keys = jax.random.split(jax.random.fold_in(seeds[10], part), 11)
    fluid_press = normal_values(part_keys[0], (FLUID_ROWS, LINE), 1.0, 6.0, ((0, 16),), jnp.float32)
    iterate = normal_values(part_keys[1], (FLUID_ROWS, LINE), 1.0, 6.0, ((0, 16),), jnp.float32)
    displace = normal_values(part_keys[2], (BLOCKS, LINE), 1.0, 6.0, ((0, 16),), jnp.float32)
    velocity = normal_values(part_keys[3], (BLOCKS, LINE), 0.5, 6.0, ((0, 16),), jnp.float32)
    stiffness = jnp.clip(jnp.exp(math.log(0.45) - 1.7272209 * jax.random.uniform(part_keys[4], (BLOCKS, LINE), jnp.float32) ** level_of(part_keys[4], (BLOCKS, LINE), ((0, 16),), -0.2, 0.2)), 0.08, 0.45)
    owners_keys = jax.random.split(jax.random.fold_in(part_keys[5], 1), BLOCKS // BLK_DEV)
    owners_turns = jax.random.permutation(jax.random.fold_in(part_keys[5], 3), BLOCKS // BLK_DEV)
    owners = jax.vmap(lambda own, number: assign_block(jax.random.fold_in(part_keys[5], 2), own, number, BLK_DEV, N_TILE, 1, MOST, 2))(owners_keys, owners_turns).reshape((BLOCKS, 1))
    diff_cur = draw_diff_cur(jax.random.fold_in(jax.random.fold_in(seeds[10], part), 71), part)
    step_cur = normal_values(part_keys[7], (CUR, FLUID_ROWS, LINE), 1.0, 6.0, ((1, 16),))
    diff_past = draw_diff_past(jax.random.fold_in(jax.random.fold_in(seeds[10], part), 71), part)
    step_past = normal_values(part_keys[9], (PAST, FLUID_ROWS, LINE), 1.0, 6.0, ((1, 16),))
    return {"fluid_press": fluid_press, "iterate": iterate, "displace": displace, "velocity": velocity, "stiffness": stiffness, "owners": owners, "diff_cur": diff_cur, "step_cur": step_cur, "diff_past": diff_past, "step_past": step_past}


step_dt = 1.0
damping = 0.05

def march(field, speed, stiffness, pressure):
    for substep in range(SUBSTEPS):
        upper = jnp.roll(field, 1, 0)
        beneath = jnp.roll(field, -1, 0)
        zero_col = jnp.zeros((field.shape[0], 1), jnp.float32)
        left = jnp.concatenate([zero_col, field[:, :-1]], 1)
        right = jnp.concatenate([field[:, 1:], zero_col], 1)
        lapl = upper + beneath + (left + right) - 4.0 * field
        speed = speed + step_dt * (stiffness * lapl + pressure - damping * speed)
        field = field + step_dt * speed
    return (field, speed)

def solve_spd(matrix, vector):
    factor = jnp.linalg.cholesky(matrix)
    inner = lax.linalg.triangular_solve(factor, vector[:, None], left_side=True, lower=True)
    outer = lax.linalg.triangular_solve(factor, inner, left_side=True, lower=True, transpose_a=True)
    return outer[:, 0]

def reference(fluid_press, iterate, displace, velocity, stiffness, owners, diff_cur, step_cur, diff_past, step_past):
    high = lax.Precision.HIGHEST
    table = owners[:, 0].reshape(N_TILE, BLK_DEV)
    onehot = (table[:, :, None] == jnp.arange(N_TILE, dtype=jnp.int32)[None, None, :]).astype(jnp.float32)
    below = (jnp.arange(BLK_DEV)[:, None] > jnp.arange(BLK_DEV)[None, :]).astype(jnp.float32)
    earlier = jnp.einsum('ij,sjn->sin', below, onehot, precision=high)
    rank_in = jnp.sum(earlier * onehot, axis=2).astype(jnp.int32)
    sources = jnp.arange(N_TILE, dtype=jnp.int32)[:, None]
    slots = (table * SLOTS_DEV + sources * MOST + rank_in).reshape(-1).astype(jnp.int32)
    mask = jnp.zeros((FLUID_ROWS,), jnp.float32).at[slots].set(1.0)
    pressure = fluid_press[slots]
    field, speed = march(displace, velocity, stiffness, pressure)
    x_tilde = jnp.zeros((FLUID_ROWS, LINE), jnp.float32).at[slots].set(field)
    resid = (mask[:, None] * (x_tilde - iterate)).astype(jnp.bfloat16)
    resid_flat = resid.astype(jnp.float32).reshape(-1)
    cur_cols = (diff_cur.astype(jnp.float32) * mask[None, :, None]).reshape(CUR, -1)
    past_cols = (diff_past.astype(jnp.float32) * mask[None, :, None]).reshape(PAST, -1)
    gram_cur = jnp.dot(cur_cols, cur_cols.T, precision=high)
    rhs_cur = jnp.dot(cur_cols, resid_flat, precision=high)
    gram_past = jnp.dot(past_cols, past_cols.T, precision=high)
    coeff = -solve_spd(gram_cur, rhs_cur)
    proj = resid_flat + jnp.dot(coeff, cur_cols, precision=high)
    past = solve_spd(gram_past, jnp.dot(past_cols, proj, precision=high))
    coeff_half = coeff.astype(jnp.bfloat16).astype(jnp.float32)
    past_half = past.astype(jnp.bfloat16).astype(jnp.float32)
    upd_cur = jnp.dot(coeff_half, step_cur.astype(jnp.float32).reshape(CUR, -1), precision=high)
    upd_past = jnp.dot(past_half, step_past.astype(jnp.float32).reshape(PAST, -1), precision=high)
    update = (upd_cur - upd_past).reshape(FLUID_ROWS, LINE)
    new_iterate = mask[:, None] * (x_tilde + update)
    return (new_iterate, field, speed)
```

```python
import functools

import jax
import jax.numpy as jnp
from jax import lax
from jax.experimental import pallas as pl
from jax.experimental.pallas import tpu as pltpu
from jax.sharding import PartitionSpec as P

SUBSTEPS = 4
DAMPING = 0.05
EDGE = 8
F32 = jnp.float32
BF16 = jnp.bfloat16


def split3(x):
    hi = x.astype(BF16)
    rest = x - hi.astype(F32)
    mid = rest.astype(BF16)
    low = (rest - mid.astype(F32)).astype(BF16)
    return hi, mid, low


def dot(a, b, dims=((1,), (0,))):
    return lax.dot_general(a, b, (dims, ((), ())), preferred_element_type=F32)


def iota(shape, axis):
    return lax.broadcasted_iota(jnp.int32, shape, axis)


def kernel(
    n, per, wide,
    press, iterate, displace, velocity, stiffness, owners, diff_cur, step_cur, diff_past, step_past,
    new_ref, field_ref, speed_ref,
    vd, vs, ext, pext, cnt, stage, pbuf, obuf, xbuf, gram, rsbuf, agbuf, prow, arbuf, elim, coefs,
    load_sem, send_sem, recv_sem, halo_send, halo_recv,
):
    me = lax.axis_index("tile")
    left, right = lax.rem(me + n - 1, n), lax.rem(me + 1, n)
    lines = displace.shape[0]
    slots = iterate.shape[0]
    nc, npast = diff_cur.shape[0], diff_past.shape[0]
    cols = vd.shape[0]
    total = n * wide

    def peers(fn):
        def step(i, carry):
            fn(lax.rem(me + i, n))
            return carry

        lax.fori_loop(1, n, step, 0)

    barrier = pltpu.get_barrier_semaphore()
    peers(lambda p: pl.semaphore_signal(
        barrier, inc=1, device_id={"tile": p}, device_id_type=pl.DeviceIdType.MESH))

    loads = [
        pltpu.make_async_copy(diff_cur, vd.at[pl.ds(0, nc)], load_sem.at[0]),
        pltpu.make_async_copy(diff_past, vd.at[pl.ds(nc, npast)], load_sem.at[1]),
        pltpu.make_async_copy(step_cur, vs.at[pl.ds(0, nc)], load_sem.at[2]),
        pltpu.make_async_copy(step_past, vs.at[pl.ds(nc, npast)], load_sem.at[3]),
    ]
    for load in loads:
        load.start()

    def send(src, dst, phase, p):
        pltpu.make_async_remote_copy(
            src_ref=src, dst_ref=dst, send_sem=send_sem.at[phase], recv_sem=recv_sem.at[phase],
            device_id={"tile": p}, device_id_type=pl.DeviceIdType.MESH).start()

    def wait(buf, sem):
        part = buf.at[pl.ds(0, n - 1)]
        pltpu.make_async_copy(part, part, sem).wait()

    ext[0, EDGE:EDGE + lines, :] = displace[...]
    ext[1, EDGE:EDGE + lines, :] = velocity[...]
    ext[2, EDGE:EDGE + lines, :] = stiffness[...]
    own = owners[...].astype(F32)
    lane_f = iota((lines, 128), 1).astype(F32)
    onehot = jnp.where(own == lane_f, 1.0, 0.0)
    cnt[me] = jnp.broadcast_to(jnp.sum(onehot, axis=0, keepdims=True), (8, 128))
    if wide != per:
        stage[...] = jnp.zeros_like(stage)
        for s in range(n):
            stage[s, 0:per, :] = press[s * per:(s + 1) * per, :]

    pl.semaphore_wait(barrier, n - 1)
    peers(lambda p: send(cnt.at[me], cnt.at[me], 0, p))

    def press_block(p):
        if wide != per:
            return stage.at[p]
        return press.at[pl.ds(pl.multiple_of(p * per, 8), per)]

    peers(lambda p: send(press_block(p), pbuf.at[me], 1, p))
    if wide != per:
        pbuf[me] = stage[me]
    else:
        pbuf[me] = press[pl.ds(pl.multiple_of(me * per, 8), per), :]

    def halos(buf, first, lead):
        moves = []
        for k, (src, dst, who) in enumerate((
            (EDGE, EDGE + lines, left),
            (lines, 0, right),
        )):
            moves.append(pltpu.make_async_remote_copy(
                src_ref=buf.at[lead + (pl.ds(src, EDGE),)], dst_ref=buf.at[lead + (pl.ds(dst, EDGE),)],
                send_sem=halo_send.at[first + k], recv_sem=halo_recv.at[first + k],
                device_id={"tile": who}, device_id_type=pl.DeviceIdType.MESH))
        for move in moves:
            move.start()
        return moves

    field_halo = halos(ext, 0, (slice(None),))

    below = jnp.where(iota((lines, lines), 0) > iota((lines, lines), 1), 1.0, 0.0).astype(BF16)
    earlier = dot(below, onehot.astype(BF16))
    rank = jnp.sum(earlier * onehot, axis=1, keepdims=True)
    slot = own * float(wide) + rank
    chooser = jnp.where(slot == iota((lines, total), 1).astype(F32), 1.0, 0.0).astype(BF16)
    same = iota((lines, lines), 0) == iota((lines, lines), 1)
    slot_row = jnp.sum(jnp.where(same, slot, 0.0), axis=0, keepdims=True)
    placer = jnp.where(slot_row == iota((total, lines), 0).astype(F32), 1.0, 0.0).astype(BF16)

    vd[nc + npast:cols] = jnp.zeros((cols - nc - npast, slots, 128), BF16)
    gram[...] = jnp.zeros_like(gram)
    prow[...] = jnp.zeros_like(prow)

    wait(cnt, recv_sem.at[0])
    mine = jnp.sum(jnp.where(iota((n, 8, 128), 2) == me, cnt[...], 0.0), axis=2, keepdims=True)
    mine = jnp.broadcast_to(mine, (n, 8, 128))
    if wide > 8:
        mine = jnp.concatenate([mine] * (wide // 8), axis=1)
    mask3 = jnp.where(iota((n, wide, 128), 1).astype(F32) < mine, 1.0, 0.0)

    def compact(cells):
        if wide == per:
            return cells.reshape(slots, 128)
        return jnp.concatenate([cells[s, 0:per, :] for s in range(n)], axis=0)

    mask = compact(mask3)
    mask_half = mask.astype(BF16)

    loads[0].wait()
    loads[1].wait()

    def apply_mask(k, carry):
        vd[k] = vd[k] * mask_half
        return carry

    lax.fori_loop(0, nc + npast, apply_mask, 0)

    def gather(a):
        return jnp.concatenate([
            vd[pl.ds(a * 16, 16), r * 16:(r + 1) * 16, :].reshape(256, 128)
            for r in range(slots // 16)], axis=1)

    def outer(a, carry):
        def inner(b, carry):
            prod = dot(gather(a), gather(b), ((1,), (1,)))
            alike = (iota((256, 256), 0) & 15) == (iota((256, 256), 1) & 15)
            kept = jnp.where(alike, prod, 0.0).reshape(16, 16, 256)
            kept = jnp.sum(kept, axis=1) * jnp.where(a == b, 0.5, 1.0)
            spread = jnp.where((iota((256, 128), 0) >> 4) + b * 16 == iota((256, 128), 1), 1.0, 0.0)
            spread = spread.astype(BF16)
            hi, mid, low = split3(kept)
            value = dot(hi, spread) + dot(mid, spread) + dot(low, spread)
            gram[pl.ds(2 * a, 2)] += value.reshape(2, 8, 128)
            return carry

        return lax.fori_loop(a, cols // 16, inner, carry)

    lax.fori_loop(0, cols // 16, outer, 0)
    peers(lambda p: send(gram.at[p], rsbuf.at[me], 2, p))
    rsbuf[me] = gram[me]

    wait(pbuf, recv_sem.at[1])
    returned = pbuf[...].reshape(total, 128)
    hi, mid, low = split3(returned)
    pext[EDGE:EDGE + lines, :] = dot(chooser, hi) + dot(chooser, mid) + dot(chooser, low)
    press_halo = halos(pext, 2, ())

    wait(rsbuf, recv_sem.at[2])
    agbuf[me] = jnp.sum(rsbuf[...], axis=0)
    peers(lambda p: send(agbuf.at[me], agbuf.at[me], 3, p))

    for move in field_halo:
        move.wait()
    for move in press_halo:
        move.wait()
    w, v, stiff, force = ext[0], ext[1], ext[2], pext[...]
    rows = lines + 2 * EDGE
    lane = iota((rows, 128), 1)
    for _ in range(SUBSTEPS):
        upper = pltpu.roll(w, 1, 0)
        beneath = pltpu.roll(w, rows - 1, 0)
        lft = jnp.where(lane == 0, 0.0, pltpu.roll(w, 1, 1))
        rgt = jnp.where(lane == 127, 0.0, pltpu.roll(w, 127, 1))
        lapl = upper + beneath + (lft + rgt) - 4.0 * w
        v = v + (stiff * lapl + force - DAMPING * v)
        w = w + v
    field = w[EDGE:EDGE + lines, :]
    hi, mid, low = split3(field)
    placed = dot(placer, hi) + dot(placer, mid) + dot(placer, low)
    obuf[...] = placed.reshape(n, wide, 128)
    peers(lambda p: send(obuf.at[p], xbuf.at[me], 4, p))
    xbuf[me] = obuf[me]
    field_ref[...] = field
    speed_ref[...] = v[EDGE:EDGE + lines, :]

    wait(agbuf, recv_sem.at[3])
    half = agbuf[0:16].reshape(128, 128)
    full = half + half.T
    lane2, sub2 = iota((nc, 128), 1), iota((nc, 128), 0)
    unit = jnp.where(lane2 == sub2 + 64, 1.0, 0.0)
    cross = full[nc:2 * nc, :]
    past_part = jnp.where(lane2 < nc, pltpu.roll(cross, 128 - nc, 1), 0.0)
    elim[0] = jnp.where(lane2 < nc, full[0:nc, :], 0.0) + unit
    elim[1] = past_part + unit + jnp.where((lane2 == sub2) & (sub2 >= npast), 1.0, 0.0)
    lane3, sub3 = iota((2, nc, 128), 2), iota((2, nc, 128), 1)

    def eliminate(j, carry):
        now = elim[...]
        row = elim[:, pl.ds(j, 1), :]
        col = jnp.sum(jnp.where(lane3 == j, now, 0.0), axis=2, keepdims=True)
        pivot = jnp.sum(jnp.where(iota((2, 1, 128), 2) == j, row, 0.0), axis=2, keepdims=True)
        elim[...] = jnp.where(sub3 > j, now - col * (row / pivot), now)
        return carry

    lax.fori_loop(0, nc, eliminate, 0)
    done = elim[...]
    diag2 = lane2 == sub2
    inverse, pivots = [], []
    for part in range(2):
        inverse.append(jnp.where(lane2 < nc, pltpu.roll(done[part], 64, 1), 0.0))
        pivots.append(jnp.sum(jnp.where(diag2, done[part], 0.0), axis=1, keepdims=True))

    wait(xbuf, recv_sem.at[4])
    x_tilde = compact(xbuf[...])
    resid = (mask * (x_tilde - iterate[...])).astype(BF16).astype(F32)

    def product(k, carry):
        prow[pl.ds(k, 1), :] = jnp.sum(vd[k].astype(F32) * resid, axis=0, keepdims=True)
        return carry

    lax.fori_loop(0, nc + npast, product, 0)
    ones = jnp.ones((8, 128), BF16)
    hi, mid, low = split3(prow[...])
    arbuf[me] = (dot(ones, hi, ((1,), (1,))) + dot(ones, mid, ((1,), (1,)))
                 + dot(ones, low, ((1,), (1,))))
    peers(lambda p: send(arbuf.at[me], arbuf.at[me], 5, p))
    loads[2].wait()
    loads[3].wait()
    wait(arbuf, recv_sem.at[5])
    rhs = jnp.sum(arbuf[...], axis=0)

    def solve(part, vector):
        inner = jnp.sum(inverse[part] * vector, axis=1, keepdims=True) / pivots[part]
        return jnp.sum(inverse[part] * inner, axis=0, keepdims=True)

    coeff = -solve(0, rhs[0:1, :])
    carried = jnp.sum(cross * coeff, axis=1, keepdims=True)
    carried = jnp.sum(jnp.where(diag2, carried, 0.0), axis=0, keepdims=True)
    past = solve(1, pltpu.roll(rhs, 128 - nc, 1)[0:1, :] + carried)
    for part, vector in enumerate((coeff, -past)):
        column = jnp.sum(jnp.where(diag2, vector, 0.0), axis=1, keepdims=True)
        coefs[part * nc:(part + 1) * nc, :] = jnp.broadcast_to(
            column, (nc, 128)).astype(BF16).astype(F32)

    def accumulate(k, acc):
        return acc + coefs[pl.ds(k, 1), :] * vs[k].astype(F32)

    update = lax.fori_loop(0, nc + npast, accumulate, jnp.zeros((slots, 128), F32))
    new_ref[...] = mask * (x_tilde + update)

    for phase, buf in enumerate((cnt, pbuf, rsbuf, agbuf, xbuf, arbuf)):
        wait(buf, send_sem.at[phase])


def local(press, iterate, displace, velocity, stiffness, owners, diff_cur, step_cur, diff_past, step_past):
    n = lax.axis_size("tile")
    lines, slots = displace.shape[0], iterate.shape[0]
    per = slots // n
    wide = max(8, per)
    nc, npast = diff_cur.shape[0], diff_past.shape[0]
    cols = -(-2 * nc // 16) * 16
    vmem = pl.BlockSpec(memory_space=pltpu.VMEM)
    hbm = pl.BlockSpec(memory_space=pl.ANY)
    tiles = pltpu.VMEM((n, 8, 128), F32)
    blocks = pltpu.VMEM((n, wide, 128), F32)
    return pl.pallas_call(
        functools.partial(kernel, n, per, wide),
        out_shape=(
            jax.ShapeDtypeStruct((slots, 128), F32),
            jax.ShapeDtypeStruct((lines, 128), F32),
            jax.ShapeDtypeStruct((lines, 128), F32),
        ),
        in_specs=[vmem] * 6 + [hbm] * 4,
        out_specs=(vmem, vmem, vmem),
        scratch_shapes=[
            pltpu.VMEM((cols, slots, 128), BF16),
            pltpu.VMEM((nc + npast, slots, 128), BF16),
            pltpu.VMEM((3, lines + 2 * EDGE, 128), F32),
            pltpu.VMEM((lines + 2 * EDGE, 128), F32),
            tiles,
            blocks if wide != per else pltpu.VMEM((8, 128), F32),
            blocks, blocks, blocks,
            tiles, tiles, tiles,
            pltpu.VMEM((128, 128), F32),
            tiles,
            pltpu.VMEM((2, nc, 128), F32),
            pltpu.VMEM((2 * nc, 128), F32),
            pltpu.SemaphoreType.DMA((4,)),
            pltpu.SemaphoreType.DMA((6,)),
            pltpu.SemaphoreType.DMA((6,)),
            pltpu.SemaphoreType.DMA((4,)),
            pltpu.SemaphoreType.DMA((4,)),
        ],
        compiler_params=pltpu.CompilerParams(
            collective_id=0, has_side_effects=True, vmem_limit_bytes=44 * 1024 * 1024),
    )(press, iterate, displace, velocity, stiffness, owners, diff_cur, step_cur, diff_past, step_past)


def solution(mesh):
    rows = P(("runs", "tile"), None)
    deep = P(None, ("runs", "tile"), None)
    return jax.shard_map(
        local,
        mesh=mesh,
        in_specs=(rows,) * 6 + (deep,) * 4,
        out_specs=(rows, rows, rows),
        check_vma=False,
    )
```

```python
import functools

import jax
import jax.numpy as jnp
from jax import lax
from jax.experimental import pallas as pl
from jax.experimental.pallas import tpu as pltpu
from jax.sharding import PartitionSpec as P

SUBSTEPS = 4
DAMPING = 0.05
EDGE = 8
F32 = jnp.float32
BF16 = jnp.bfloat16


def split3(x):
    hi = x.astype(BF16)
    rest = x - hi.astype(F32)
    mid = rest.astype(BF16)
    low = (rest - mid.astype(F32)).astype(BF16)
    return hi, mid, low


def dot(a, b, dims=((1,), (0,))):
    return lax.dot_general(a, b, (dims, ((), ())), preferred_element_type=F32)


def iota(shape, axis):
    return lax.broadcasted_iota(jnp.int32, shape, axis)


def kernel(
    n, per, wide,
    press, iterate, displace, velocity, stiffness, owners, diff_cur, step_cur, diff_past, step_past,
    new_ref, field_ref, speed_ref,
    vd, vs, masked, halfmask, iter_v, own_v, ext, pext, cnt, raw, stage, pbuf, obuf, xbuf, gram, rsbuf, agbuf, prow, arbuf, elim, coefs,
    load_sem, small_sem, send_sem, recv_sem, halo_send, halo_recv,
):
    me = lax.axis_index("tile")
    left, right = lax.rem(me + n - 1, n), lax.rem(me + 1, n)
    lines = displace.shape[0]
    slots = iterate.shape[0]
    nc, npast = diff_cur.shape[0], diff_past.shape[0]
    cols = vd.shape[0]
    total = n * wide

    def peers(fn):
        def step(i, carry):
            fn(lax.rem(me + i, n))
            return carry

        lax.fori_loop(1, n, step, 0)

    barrier = pltpu.get_barrier_semaphore()
    peers(lambda p: pl.semaphore_signal(
        barrier, inc=1, device_id={"tile": p}, device_id_type=pl.DeviceIdType.MESH))

    loads = [
        pltpu.make_async_copy(diff_cur, vd.at[pl.ds(0, nc)], load_sem.at[0]),
        pltpu.make_async_copy(diff_past, vd.at[pl.ds(nc, npast)], load_sem.at[1]),
        pltpu.make_async_copy(step_cur, vs.at[pl.ds(0, nc)], load_sem.at[2]),
        pltpu.make_async_copy(step_past, vs.at[pl.ds(nc, npast)], load_sem.at[3]),
    ]
    small = [
        pltpu.make_async_copy(owners, own_v, small_sem.at[0]),
        pltpu.make_async_copy(displace, ext.at[0, pl.ds(EDGE, lines)], small_sem.at[1]),
        pltpu.make_async_copy(velocity, ext.at[1, pl.ds(EDGE, lines)], small_sem.at[2]),
        pltpu.make_async_copy(stiffness, ext.at[2, pl.ds(EDGE, lines)], small_sem.at[3]),
        pltpu.make_async_copy(iterate, iter_v, small_sem.at[4]),
    ]
    if wide != per:
        small.append(pltpu.make_async_copy(press, raw, small_sem.at[5]))
    else:
        small.append(pltpu.make_async_copy(
            press.at[pl.ds(pl.multiple_of(me * per, 8), per)], pbuf.at[me], small_sem.at[5]))
    for load in small + loads:
        load.start()

    def send(src, dst, phase, p):
        pltpu.make_async_remote_copy(
            src_ref=src, dst_ref=dst, send_sem=send_sem.at[phase], recv_sem=recv_sem.at[phase],
            device_id={"tile": p}, device_id_type=pl.DeviceIdType.MESH).start()

    def wait(buf, sem):
        part = buf.at[pl.ds(0, n - 1)]
        pltpu.make_async_copy(part, part, sem).wait()

    vd[nc + npast:cols] = jnp.zeros((cols - nc - npast, slots, 128), BF16)
    gram[...] = jnp.zeros_like(gram)
    prow[...] = jnp.zeros_like(prow)
    small[0].wait()
    same = iota((lines, lines), 0) == iota((lines, lines), 1)
    own_row = jnp.broadcast_to(own_v[...].astype(F32), (lines, lines))
    own = jnp.sum(jnp.where(same, own_row, 0.0), axis=1, keepdims=True)
    lane_f = iota((lines, 128), 1).astype(F32)
    onehot = jnp.where(own == lane_f, 1.0, 0.0)
    cnt[me] = jnp.broadcast_to(jnp.sum(onehot, axis=0, keepdims=True), (8, 128))
    if wide != per:
        small[5].wait()
        stage[...] = jnp.zeros_like(stage)
        for s in range(n):
            stage[s, 0:per, :] = raw[s * per:(s + 1) * per, :]

    pl.semaphore_wait(barrier, n - 1)
    peers(lambda p: send(cnt.at[me], cnt.at[me], 0, p))

    def press_block(p):
        if wide != per:
            return stage.at[p]
        return press.at[pl.ds(pl.multiple_of(p * per, 8), per)]

    peers(lambda p: send(press_block(p), pbuf.at[me], 1, p))
    if wide != per:
        pbuf[me] = stage[me]

    def halos(buf, first, lead):
        moves = []
        for k, (src, dst, who) in enumerate((
            (EDGE, EDGE + lines, left),
            (lines, 0, right),
        )):
            moves.append(pltpu.make_async_remote_copy(
                src_ref=buf.at[lead + (pl.ds(src, EDGE),)], dst_ref=buf.at[lead + (pl.ds(dst, EDGE),)],
                send_sem=halo_send.at[first + k], recv_sem=halo_recv.at[first + k],
                device_id={"tile": who}, device_id_type=pl.DeviceIdType.MESH))
        for move in moves:
            move.start()
        return moves

    for load in small[1:4]:
        load.wait()
    field_halo = halos(ext, 0, (slice(None),))

    below = jnp.where(iota((lines, lines), 0) > iota((lines, lines), 1), 1.0, 0.0).astype(BF16)
    earlier = dot(below, onehot.astype(BF16))
    rank = jnp.sum(earlier * onehot, axis=1, keepdims=True)
    slot = own * float(wide) + rank
    chooser = jnp.where(slot == iota((lines, total), 1).astype(F32), 1.0, 0.0).astype(BF16)
    slot_row = jnp.sum(jnp.where(same, slot, 0.0), axis=0, keepdims=True)
    placer = jnp.where(slot_row == iota((total, lines), 0).astype(F32), 1.0, 0.0).astype(BF16)

    wait(cnt, recv_sem.at[0])
    mine = jnp.sum(jnp.where(iota((n, 8, 128), 2) == me, cnt[...], 0.0), axis=2, keepdims=True)
    mine = jnp.broadcast_to(mine, (n, 8, 128))
    if wide > 8:
        mine = jnp.concatenate([mine] * (wide // 8), axis=1)
    mask3 = jnp.where(iota((n, wide, 128), 1).astype(F32) < mine, 1.0, 0.0)

    def compact(cells):
        if wide == per:
            return cells.reshape(slots, 128)
        return jnp.concatenate([cells[s, 0:per, :] for s in range(n)], axis=0)

    mask = compact(mask3)
    halfmask[...] = mask.astype(BF16)

    loads[0].wait()
    loads[1].wait()

    def gather(a):
        return jnp.concatenate([
            vd[pl.ds(a * 16, 16), r * 16:(r + 1) * 16, :].reshape(256, 128)
            for r in range(slots // 16)], axis=1)

    def outer(a, carry):
        for r in range(slots // 16):
            rows16 = slice(r * 16, (r + 1) * 16)
            block = vd[pl.ds(a * 16, 16), rows16, :] * halfmask[rows16, :][None]
            masked[:, r * 128:(r + 1) * 128] = block.reshape(256, 128)

        def inner(b, carry):
            prod = dot(masked[...], gather(b), ((1,), (1,)))
            alike = (iota((256, 256), 0) & 15) == (iota((256, 256), 1) & 15)
            kept = jnp.where(alike, prod, 0.0).reshape(16, 16, 256)
            kept = jnp.sum(kept, axis=1) * jnp.where(a == b, 0.5, 1.0)
            spread = jnp.where((iota((256, 128), 0) >> 4) + b * 16 == iota((256, 128), 1), 1.0, 0.0)
            spread = spread.astype(BF16)
            hi, mid, low = split3(kept)
            value = dot(hi, spread) + dot(mid, spread) + dot(low, spread)
            gram[pl.ds(2 * a, 2)] += value.reshape(2, 8, 128)
            return carry

        return lax.fori_loop(a, cols // 16, inner, carry)

    lax.fori_loop(0, 1, outer, 0)

    wait(pbuf, recv_sem.at[1])
    if wide == per:
        small[5].wait()
    returned = pbuf[...].reshape(total, 128)
    hi, mid, low = split3(returned)
    pext[EDGE:EDGE + lines, :] = dot(chooser, hi) + dot(chooser, mid) + dot(chooser, low)
    press_halo = halos(pext, 2, ())

    lax.fori_loop(1, 2, outer, 0)

    for move in field_halo:
        move.wait()
    for move in press_halo:
        move.wait()
    w, v, stiff, force = ext[0], ext[1], ext[2], pext[...]
    rows = lines + 2 * EDGE
    lane = iota((rows, 128), 1)
    for _ in range(SUBSTEPS):
        upper = pltpu.roll(w, 1, 0)
        beneath = pltpu.roll(w, rows - 1, 0)
        lft = jnp.where(lane == 0, 0.0, pltpu.roll(w, 1, 1))
        rgt = jnp.where(lane == 127, 0.0, pltpu.roll(w, 127, 1))
        lapl = upper + beneath + (lft + rgt) - 4.0 * w
        v = v + (stiff * lapl + force - DAMPING * v)
        w = w + v
    field = w[EDGE:EDGE + lines, :]
    hi, mid, low = split3(field)
    placed = dot(placer, hi) + dot(placer, mid) + dot(placer, low)
    obuf[...] = placed.reshape(n, wide, 128)
    peers(lambda p: send(obuf.at[p], xbuf.at[me], 4, p))
    xbuf[me] = obuf[me]
    field_ref[...] = field
    speed_ref[...] = v[EDGE:EDGE + lines, :]

    lax.fori_loop(2, cols // 16, outer, 0)
    peers(lambda p: send(gram.at[p], rsbuf.at[me], 2, p))
    rsbuf[me] = gram[me]

    wait(xbuf, recv_sem.at[4])
    small[4].wait()
    x_tilde = compact(xbuf[...])
    resid = (mask * (x_tilde - iter_v[...])).astype(BF16).astype(F32)

    def product(k, carry):
        for u in range(10):
            prow[pl.ds(k * 10 + u, 1), :] = jnp.sum(
                vd[k * 10 + u].astype(F32) * resid, axis=0, keepdims=True)
        return carry

    lax.fori_loop(0, (nc + npast) // 10, product, 0)
    ones = jnp.ones((8, 128), BF16)
    hi, mid, low = split3(prow[...])
    arbuf[me] = (dot(ones, hi, ((1,), (1,))) + dot(ones, mid, ((1,), (1,)))
                 + dot(ones, low, ((1,), (1,))))
    peers(lambda p: send(arbuf.at[me], arbuf.at[me], 5, p))
    wait(rsbuf, recv_sem.at[2])
    agbuf[me] = jnp.sum(rsbuf[...], axis=0)
    peers(lambda p: send(agbuf.at[me], agbuf.at[me], 3, p))

    wait(agbuf, recv_sem.at[3])
    half = agbuf[0:16].reshape(128, 128)
    full = half + half.T
    lane2, sub2 = iota((nc, 128), 1), iota((nc, 128), 0)
    unit = jnp.where(lane2 == sub2 + 64, 1.0, 0.0)
    cross = full[nc:2 * nc, :]
    past_part = jnp.where(lane2 < nc, pltpu.roll(cross, 128 - nc, 1), 0.0)
    elim[0] = jnp.where(lane2 < nc, full[0:nc, :], 0.0) + unit
    elim[1] = past_part + unit + jnp.where((lane2 == sub2) & (sub2 >= npast), 1.0, 0.0)
    lane3, sub3 = iota((2, nc, 128), 2), iota((2, nc, 128), 1)

    def eliminate(j, carry):
        now = elim[...]
        row = elim[:, pl.ds(j, 1), :]
        col = jnp.sum(jnp.where(lane3 == j, now, 0.0), axis=2, keepdims=True)
        pivot = jnp.sum(jnp.where(iota((2, 1, 128), 2) == j, row, 0.0), axis=2, keepdims=True)
        elim[...] = jnp.where(sub3 > j, now - col * (row / pivot), now)
        return carry

    lax.fori_loop(0, nc, eliminate, 0)
    done = elim[...]
    diag2 = lane2 == sub2
    inverse, pivots = [], []
    for part in range(2):
        inverse.append(jnp.where(lane2 < nc, pltpu.roll(done[part], 64, 1), 0.0))
        pivots.append(jnp.sum(jnp.where(diag2, done[part], 0.0), axis=1, keepdims=True))

    loads[2].wait()
    loads[3].wait()
    wait(arbuf, recv_sem.at[5])
    rhs = jnp.sum(arbuf[...], axis=0)

    def solve(part, vector):
        inner = jnp.sum(inverse[part] * vector, axis=1, keepdims=True) / pivots[part]
        return jnp.sum(inverse[part] * inner, axis=0, keepdims=True)

    coeff = -solve(0, rhs[0:1, :])
    carried = jnp.sum(cross * coeff, axis=1, keepdims=True)
    carried = jnp.sum(jnp.where(diag2, carried, 0.0), axis=0, keepdims=True)
    past = solve(1, pltpu.roll(rhs, 128 - nc, 1)[0:1, :] + carried)
    for part, vector in enumerate((coeff, -past)):
        column = jnp.sum(jnp.where(diag2, vector, 0.0), axis=1, keepdims=True)
        coefs[part * nc:(part + 1) * nc, :] = jnp.broadcast_to(
            column, (nc, 128)).astype(BF16).astype(F32)

    def accumulate(k, acc):
        for u in range(10):
            acc = acc + coefs[pl.ds(k * 10 + u, 1), :] * vs[k * 10 + u].astype(F32)
        return acc

    update = lax.fori_loop(0, (nc + npast) // 10, accumulate, jnp.zeros((slots, 128), F32))
    new_ref[...] = mask * (x_tilde + update)

    for phase, buf in enumerate((cnt, pbuf, rsbuf, agbuf, xbuf, arbuf)):
        wait(buf, send_sem.at[phase])


def hand_over(a, b, c, a_out, b_out, c_out, sems):
    moves = [pltpu.make_async_copy(src, dst, sems.at[i])
             for i, (src, dst) in enumerate(((a, a_out), (b, b_out), (c, c_out)))]
    for move in moves:
        move.start()
    for move in moves:
        move.wait()


def local(press, iterate, displace, velocity, stiffness, owners, diff_cur, step_cur, diff_past, step_past):
    n = lax.axis_size("tile")
    lines, slots = displace.shape[0], iterate.shape[0]
    per = slots // n
    wide = max(8, per)
    nc, npast = diff_cur.shape[0], diff_past.shape[0]
    cols = -(-2 * nc // 16) * 16
    vmem = pl.BlockSpec(memory_space=pltpu.VMEM)
    hbm = pl.BlockSpec(memory_space=pl.ANY)
    tiles = pltpu.VMEM((n, 8, 128), F32)
    blocks = pltpu.VMEM((n, wide, 128), F32)
    outs = pl.pallas_call(
        functools.partial(kernel, n, per, wide),
        out_shape=(
            jax.ShapeDtypeStruct((slots, 128), F32),
            jax.ShapeDtypeStruct((lines, 128), F32),
            jax.ShapeDtypeStruct((lines, 128), F32),
        ),
        in_specs=[hbm] * 10,
        out_specs=(vmem, vmem, vmem),
        scratch_shapes=[
            pltpu.VMEM((cols, slots, 128), BF16),
            pltpu.VMEM((nc + npast, slots, 128), BF16),
            pltpu.VMEM((256, slots // 16 * 128), BF16),
            pltpu.VMEM((slots, 128), BF16),
            pltpu.VMEM((slots, 128), F32),
            pltpu.VMEM((1, lines), jnp.int32),
            pltpu.VMEM((3, lines + 2 * EDGE, 128), F32),
            pltpu.VMEM((lines + 2 * EDGE, 128), F32),
            tiles,
            pltpu.VMEM((slots if wide != per else 8, 128), F32),
            blocks if wide != per else pltpu.VMEM((8, 128), F32),
            blocks, blocks, blocks,
            tiles, tiles, tiles,
            pltpu.VMEM((128, 128), F32),
            tiles,
            pltpu.VMEM((2, nc, 128), F32),
            pltpu.VMEM((2 * nc, 128), F32),
            pltpu.SemaphoreType.DMA((4,)),
            pltpu.SemaphoreType.DMA((6,)),
            pltpu.SemaphoreType.DMA((6,)),
            pltpu.SemaphoreType.DMA((6,)),
            pltpu.SemaphoreType.DMA((4,)),
            pltpu.SemaphoreType.DMA((4,)),
        ],
        compiler_params=pltpu.CompilerParams(
            collective_id=0, has_side_effects=True, vmem_limit_bytes=62 * 1024 * 1024),
    )(press, iterate, displace, velocity, stiffness, owners.reshape(1, lines),
      diff_cur, step_cur, diff_past, step_past)
    return pl.pallas_call(
        hand_over,
        out_shape=tuple(jax.ShapeDtypeStruct(out.shape, out.dtype) for out in outs),
        in_specs=[hbm] * 3,
        out_specs=(hbm,) * 3,
        scratch_shapes=[pltpu.SemaphoreType.DMA((3,))],
        compiler_params=pltpu.CompilerParams(vmem_limit_bytes=62 * 1024 * 1024),
    )(*outs)


def solution(mesh):
    rows = P(("runs", "tile"), None)
    deep = P(None, ("runs", "tile"), None)
    return jax.shard_map(
        local,
        mesh=mesh,
        in_specs=(rows,) * 6 + (deep,) * 4,
        out_specs=(rows, rows, rows),
        check_vma=False,
    )
```

```python
import functools

import jax
import jax.numpy as jnp
from jax import lax
from jax.experimental import pallas as pl
from jax.experimental.pallas import tpu as pltpu
from jax.sharding import PartitionSpec as P

SUBSTEPS = 4
DAMPING = 0.05
EDGE = 8
F32 = jnp.float32
BF16 = jnp.bfloat16


def split3(x):
    hi = x.astype(BF16)
    rest = x - hi.astype(F32)
    mid = rest.astype(BF16)
    low = (rest - mid.astype(F32)).astype(BF16)
    return hi, mid, low


def dot(a, b, dims=((1,), (0,))):
    return lax.dot_general(a, b, (dims, ((), ())), preferred_element_type=F32)


def iota(shape, axis):
    return lax.broadcasted_iota(jnp.int32, shape, axis)


def kernel(
    n, per, wide,
    press, iterate, displace, velocity, stiffness, owners, diff_cur, step_cur, diff_past, step_past,
    new_ref, field_ref, speed_ref,
    vd, vs, masked, kbuf, halfmask, iter_v, own_v, ext, pext, cnt, raw, stage, pbuf, obuf, xbuf, gram, rsbuf, agbuf, prow, arbuf, elim, coefs,
    load_sem, small_sem, send_sem, recv_sem, halo_send, halo_recv,
):
    me = lax.axis_index("tile")
    left, right = lax.rem(me + n - 1, n), lax.rem(me + 1, n)
    lines = displace.shape[0]
    slots = iterate.shape[0]
    nc, npast = diff_cur.shape[0], diff_past.shape[0]
    cols = vd.shape[0]
    total = n * wide

    def peers(fn):
        def step(i, carry):
            fn(lax.rem(me + i, n))
            return carry

        lax.fori_loop(1, n, step, 0)

    barrier = pltpu.get_barrier_semaphore()
    peers(lambda p: pl.semaphore_signal(
        barrier, inc=1, device_id={"tile": p}, device_id_type=pl.DeviceIdType.MESH))

    loads = [
        pltpu.make_async_copy(diff_cur, vd.at[pl.ds(0, nc)], load_sem.at[0]),
        pltpu.make_async_copy(diff_past, vd.at[pl.ds(nc, npast)], load_sem.at[1]),
        pltpu.make_async_copy(step_cur, vs.at[pl.ds(0, nc)], load_sem.at[2]),
        pltpu.make_async_copy(step_past, vs.at[pl.ds(nc, npast)], load_sem.at[3]),
    ]
    small = [
        pltpu.make_async_copy(owners, own_v, small_sem.at[0]),
        pltpu.make_async_copy(displace, ext.at[0, pl.ds(EDGE, lines)], small_sem.at[1]),
        pltpu.make_async_copy(velocity, ext.at[1, pl.ds(EDGE, lines)], small_sem.at[2]),
        pltpu.make_async_copy(stiffness, ext.at[2, pl.ds(EDGE, lines)], small_sem.at[3]),
        pltpu.make_async_copy(iterate, iter_v, small_sem.at[4]),
    ]
    if wide != per:
        small.append(pltpu.make_async_copy(press, raw, small_sem.at[5]))
    else:
        small.append(pltpu.make_async_copy(
            press.at[pl.ds(pl.multiple_of(me * per, 8), per)], pbuf.at[me], small_sem.at[5]))
    for load in small + loads:
        load.start()

    def send(src, dst, phase, p):
        pltpu.make_async_remote_copy(
            src_ref=src, dst_ref=dst, send_sem=send_sem.at[phase], recv_sem=recv_sem.at[phase],
            device_id={"tile": p}, device_id_type=pl.DeviceIdType.MESH).start()

    def wait(buf, sem):
        part = buf.at[pl.ds(0, n - 1)]
        pltpu.make_async_copy(part, part, sem).wait()

    vd[nc + npast:cols] = jnp.zeros((cols - nc - npast, slots, 128), BF16)
    gram[...] = jnp.zeros_like(gram)
    kbuf[...] = jnp.zeros_like(kbuf)
    prow[...] = jnp.zeros_like(prow)
    small[0].wait()
    same = iota((lines, lines), 0) == iota((lines, lines), 1)
    own_row = jnp.broadcast_to(own_v[...].astype(F32), (lines, lines))
    own = jnp.sum(jnp.where(same, own_row, 0.0), axis=1, keepdims=True)
    lane_f = iota((lines, 128), 1).astype(F32)
    onehot = jnp.where(own == lane_f, 1.0, 0.0)
    cnt[me] = jnp.broadcast_to(jnp.sum(onehot, axis=0, keepdims=True), (8, 128))
    if wide != per:
        small[5].wait()
        stage[...] = jnp.zeros_like(stage)
        for s in range(n):
            stage[s, 0:per, :] = raw[s * per:(s + 1) * per, :]

    pl.semaphore_wait(barrier, n - 1)
    peers(lambda p: send(cnt.at[me], cnt.at[me], 0, p))

    def press_block(p):
        if wide != per:
            return stage.at[p]
        return press.at[pl.ds(pl.multiple_of(p * per, 8), per)]

    peers(lambda p: send(press_block(p), pbuf.at[me], 1, p))
    if wide != per:
        pbuf[me] = stage[me]

    def halos(buf, first, lead):
        moves = []
        for k, (src, dst, who) in enumerate((
            (EDGE, EDGE + lines, left),
            (lines, 0, right),
        )):
            moves.append(pltpu.make_async_remote_copy(
                src_ref=buf.at[lead + (pl.ds(src, EDGE),)], dst_ref=buf.at[lead + (pl.ds(dst, EDGE),)],
                send_sem=halo_send.at[first + k], recv_sem=halo_recv.at[first + k],
                device_id={"tile": who}, device_id_type=pl.DeviceIdType.MESH))
        for move in moves:
            move.start()
        return moves

    for load in small[1:4]:
        load.wait()
    field_halo = halos(ext, 0, (slice(None),))

    below = jnp.where(iota((lines, lines), 0) > iota((lines, lines), 1), 1.0, 0.0).astype(BF16)
    earlier = dot(below, onehot.astype(BF16))
    rank = jnp.sum(earlier * onehot, axis=1, keepdims=True)
    slot = own * float(wide) + rank
    chooser = jnp.where(slot == iota((lines, total), 1).astype(F32), 1.0, 0.0).astype(BF16)
    slot_row = jnp.sum(jnp.where(same, slot, 0.0), axis=0, keepdims=True)
    placer = jnp.where(slot_row == iota((total, lines), 0).astype(F32), 1.0, 0.0).astype(BF16)

    wait(cnt, recv_sem.at[0])
    mine = jnp.sum(jnp.where(iota((n, 8, 128), 2) == me, cnt[...], 0.0), axis=2, keepdims=True)
    mine = jnp.broadcast_to(mine, (n, 8, 128))
    if wide > 8:
        mine = jnp.concatenate([mine] * (wide // 8), axis=1)
    mask3 = jnp.where(iota((n, wide, 128), 1).astype(F32) < mine, 1.0, 0.0)

    def compact(cells):
        if wide == per:
            return cells.reshape(slots, 128)
        return jnp.concatenate([cells[s, 0:per, :] for s in range(n)], axis=0)

    mask = compact(mask3)
    halfmask[...] = mask.astype(BF16)

    loads[0].wait()
    loads[1].wait()

    def gather(a):
        return jnp.concatenate([
            vd[pl.ds(a * 16, 16), r * 16:(r + 1) * 16, :].reshape(256, 128)
            for r in range(slots // 16)], axis=1)

    def outer(a, carry):
        for r in range(slots // 16):
            rows16 = slice(r * 16, (r + 1) * 16)
            block = vd[pl.ds(a * 16, 16), rows16, :] * halfmask[rows16, :][None]
            masked[:, r * 128:(r + 1) * 128] = block.reshape(256, 128)

        def inner(b, carry):
            prod = dot(masked[...], gather(b), ((1,), (1,)))
            alike = (iota((256, 256), 0) & 15) == (iota((256, 256), 1) & 15)
            kept = jnp.where(alike, prod, 0.0).reshape(16, 16, 256)
            kept = jnp.sum(kept, axis=1) * jnp.where(a == b, 0.5, 1.0)
            kbuf[pl.ds(pl.multiple_of(a * 16, 16), 16), pl.ds(pl.multiple_of(b * 256, 256), 256)] = kept
            return carry

        return lax.fori_loop(a, cols // 16, inner, carry)

    lax.fori_loop(0, 1, outer, 0)

    wait(pbuf, recv_sem.at[1])
    if wide == per:
        small[5].wait()
    returned = pbuf[...].reshape(total, 128)
    hi, mid, low = split3(returned)
    pext[EDGE:EDGE + lines, :] = dot(chooser, hi) + dot(chooser, mid) + dot(chooser, low)
    press_halo = halos(pext, 2, ())

    lax.fori_loop(1, 2, outer, 0)

    for move in field_halo:
        move.wait()
    for move in press_halo:
        move.wait()
    w, v, stiff, force = ext[0], ext[1], ext[2], pext[...]
    rows = lines + 2 * EDGE
    lane = iota((rows, 128), 1)
    for _ in range(SUBSTEPS):
        upper = pltpu.roll(w, 1, 0)
        beneath = pltpu.roll(w, rows - 1, 0)
        lft = jnp.where(lane == 0, 0.0, pltpu.roll(w, 1, 1))
        rgt = jnp.where(lane == 127, 0.0, pltpu.roll(w, 127, 1))
        lapl = upper + beneath + (lft + rgt) - 4.0 * w
        v = v + (stiff * lapl + force - DAMPING * v)
        w = w + v
    field = w[EDGE:EDGE + lines, :]
    hi, mid, low = split3(field)
    placed = dot(placer, hi) + dot(placer, mid) + dot(placer, low)
    obuf[...] = placed.reshape(n, wide, 128)
    peers(lambda p: send(obuf.at[p], xbuf.at[me], 4, p))
    xbuf[me] = obuf[me]
    field_ref[...] = field
    speed_ref[...] = v[EDGE:EDGE + lines, :]

    lax.fori_loop(2, cols // 16, outer, 0)
    spread = jnp.where((iota((cols * 16, 128), 0) >> 4) == iota((cols * 16, 128), 1), 1.0, 0.0)
    spread = spread.astype(BF16)
    hi, mid, low = split3(kbuf[...])
    value = dot(hi, spread) + dot(mid, spread) + dot(low, spread)
    gram[0:cols // 8] = value.reshape(cols // 8, 8, 128)
    peers(lambda p: send(gram.at[p], rsbuf.at[me], 2, p))
    rsbuf[me] = gram[me]

    wait(xbuf, recv_sem.at[4])
    small[4].wait()
    x_tilde = compact(xbuf[...])
    resid = (mask * (x_tilde - iter_v[...])).astype(BF16).astype(F32)

    def product(k, carry):
        for u in range(10):
            prow[pl.ds(k * 10 + u, 1), :] = jnp.sum(
                vd[k * 10 + u].astype(F32) * resid, axis=0, keepdims=True)
        return carry

    lax.fori_loop(0, (nc + npast) // 10, product, 0)
    ones = jnp.ones((8, 128), BF16)
    hi, mid, low = split3(prow[...])
    arbuf[me] = (dot(ones, hi, ((1,), (1,))) + dot(ones, mid, ((1,), (1,)))
                 + dot(ones, low, ((1,), (1,))))
    peers(lambda p: send(arbuf.at[me], arbuf.at[me], 5, p))
    wait(rsbuf, recv_sem.at[2])
    agbuf[me] = jnp.sum(rsbuf[...], axis=0)
    peers(lambda p: send(agbuf.at[me], agbuf.at[me], 3, p))

    wait(agbuf, recv_sem.at[3])
    half = agbuf[0:16].reshape(128, 128)
    full = half + half.T
    lane2, sub2 = iota((nc, 128), 1), iota((nc, 128), 0)
    unit = jnp.where(lane2 == sub2 + 64, 1.0, 0.0)
    cross = full[nc:2 * nc, :]
    past_part = jnp.where(lane2 < nc, pltpu.roll(cross, 128 - nc, 1), 0.0)
    elim[0] = jnp.where(lane2 < nc, full[0:nc, :], 0.0) + unit
    elim[1] = past_part + unit + jnp.where((lane2 == sub2) & (sub2 >= npast), 1.0, 0.0)
    lane3, sub3 = iota((2, nc, 128), 2), iota((2, nc, 128), 1)

    lane1 = iota((2, 1, 128), 2)

    def eliminate(i, carry):
        j = 2 * i
        now = elim[...]
        row0, row1 = elim[:, pl.ds(j, 1), :], elim[:, pl.ds(j + 1, 1), :]
        col0 = jnp.sum(jnp.where(lane3 == j, now, 0.0), axis=2, keepdims=True)
        col1 = jnp.sum(jnp.where(lane3 == j + 1, now, 0.0), axis=2, keepdims=True)
        top = jnp.sum(jnp.where(lane1 == j, row0, 0.0), axis=2, keepdims=True)
        side = jnp.sum(jnp.where(lane1 == j, row1, 0.0), axis=2, keepdims=True)
        corner = jnp.sum(jnp.where(lane1 == j + 1, row1, 0.0), axis=2, keepdims=True)
        factor = side / top
        row1 = row1 - factor * row0
        col1 = col1 - factor * col0
        corner = corner - factor * side
        later = now - col0 * (row0 / top) - col1 * (row1 / corner)
        elim[...] = jnp.where(sub3 > j + 1, later, jnp.where(sub3 == j + 1, row1, now))
        return carry

    lax.fori_loop(0, nc // 2, eliminate, 0)
    done = elim[...]
    diag2 = lane2 == sub2
    inverse, pivots = [], []
    for part in range(2):
        inverse.append(jnp.where(lane2 < nc, pltpu.roll(done[part], 64, 1), 0.0))
        pivots.append(jnp.sum(jnp.where(diag2, done[part], 0.0), axis=1, keepdims=True))

    loads[2].wait()
    loads[3].wait()
    wait(arbuf, recv_sem.at[5])
    rhs = jnp.sum(arbuf[...], axis=0)

    def solve(part, vector):
        inner = jnp.sum(inverse[part] * vector, axis=1, keepdims=True) / pivots[part]
        return jnp.sum(inverse[part] * inner, axis=0, keepdims=True)

    coeff = -solve(0, rhs[0:1, :])
    carried = jnp.sum(cross * coeff, axis=1, keepdims=True)
    carried = jnp.sum(jnp.where(diag2, carried, 0.0), axis=0, keepdims=True)
    past = solve(1, pltpu.roll(rhs, 128 - nc, 1)[0:1, :] + carried)
    for part, vector in enumerate((coeff, -past)):
        column = jnp.sum(jnp.where(diag2, vector, 0.0), axis=1, keepdims=True)
        coefs[part * nc:(part + 1) * nc, :] = jnp.broadcast_to(
            column, (nc, 128)).astype(BF16).astype(F32)

    def accumulate(k, acc):
        for u in range(10):
            acc = acc + coefs[pl.ds(k * 10 + u, 1), :] * vs[k * 10 + u].astype(F32)
        return acc

    update = lax.fori_loop(0, (nc + npast) // 10, accumulate, jnp.zeros((slots, 128), F32))
    new_ref[...] = mask * (x_tilde + update)

    for phase, buf in enumerate((cnt, pbuf, rsbuf, agbuf, xbuf, arbuf)):
        wait(buf, send_sem.at[phase])


def hand_over(a, b, c, a_out, b_out, c_out, a_held, b_held, c_held, sems):
    pairs = ((a, a_held, a_out), (b, b_held, b_out), (c, c_held, c_out))
    fetch = [pltpu.make_async_copy(src, held, sems.at[0, i]) for i, (src, held, _) in enumerate(pairs)]
    store = [pltpu.make_async_copy(held, dst, sems.at[1, i]) for i, (_, held, dst) in enumerate(pairs)]
    for move in fetch:
        move.start()
    for move, after in zip(fetch, store):
        move.wait()
        after.start()
    for move in store:
        move.wait()


def local(press, iterate, displace, velocity, stiffness, owners, diff_cur, step_cur, diff_past, step_past):
    n = lax.axis_size("tile")
    lines, slots = displace.shape[0], iterate.shape[0]
    per = slots // n
    wide = max(8, per)
    nc, npast = diff_cur.shape[0], diff_past.shape[0]
    cols = -(-2 * nc // 16) * 16
    vmem = pl.BlockSpec(memory_space=pltpu.VMEM)
    hbm = pl.BlockSpec(memory_space=pl.ANY)
    tiles = pltpu.VMEM((n, 8, 128), F32)
    blocks = pltpu.VMEM((n, wide, 128), F32)
    outs = pl.pallas_call(
        functools.partial(kernel, n, per, wide),
        out_shape=(
            jax.ShapeDtypeStruct((slots, 128), F32),
            jax.ShapeDtypeStruct((lines, 128), F32),
            jax.ShapeDtypeStruct((lines, 128), F32),
        ),
        in_specs=[hbm] * 10,
        out_specs=(vmem, vmem, vmem),
        scratch_shapes=[
            pltpu.VMEM((cols, slots, 128), BF16),
            pltpu.VMEM((nc + npast, slots, 128), BF16),
            pltpu.VMEM((256, slots // 16 * 128), BF16),
            pltpu.VMEM((cols, cols * 16), F32),
            pltpu.VMEM((slots, 128), BF16),
            pltpu.VMEM((slots, 128), F32),
            pltpu.VMEM((1, lines), jnp.int32),
            pltpu.VMEM((3, lines + 2 * EDGE, 128), F32),
            pltpu.VMEM((lines + 2 * EDGE, 128), F32),
            tiles,
            pltpu.VMEM((slots if wide != per else 8, 128), F32),
            blocks if wide != per else pltpu.VMEM((8, 128), F32),
            blocks, blocks, blocks,
            tiles, tiles, tiles,
            pltpu.VMEM((128, 128), F32),
            tiles,
            pltpu.VMEM((2, nc, 128), F32),
            pltpu.VMEM((2 * nc, 128), F32),
            pltpu.SemaphoreType.DMA((4,)),
            pltpu.SemaphoreType.DMA((6,)),
            pltpu.SemaphoreType.DMA((6,)),
            pltpu.SemaphoreType.DMA((6,)),
            pltpu.SemaphoreType.DMA((4,)),
            pltpu.SemaphoreType.DMA((4,)),
        ],
        compiler_params=pltpu.CompilerParams(
            collective_id=0, has_side_effects=True, vmem_limit_bytes=62 * 1024 * 1024),
    )(press, iterate, displace, velocity, stiffness, owners.reshape(1, lines),
      diff_cur, step_cur, diff_past, step_past)
    return pl.pallas_call(
        hand_over,
        out_shape=tuple(jax.ShapeDtypeStruct(out.shape, out.dtype) for out in outs),
        in_specs=[hbm] * 3,
        out_specs=(hbm,) * 3,
        scratch_shapes=[pltpu.VMEM(out.shape, out.dtype) for out in outs]
        + [pltpu.SemaphoreType.DMA((2, 3))],
        compiler_params=pltpu.CompilerParams(vmem_limit_bytes=62 * 1024 * 1024),
    )(*outs)


def solution(mesh):
    rows = P(("runs", "tile"), None)
    deep = P(None, ("runs", "tile"), None)
    return jax.shard_map(
        local,
        mesh=mesh,
        in_specs=(rows,) * 6 + (deep,) * 4,
        out_specs=(rows, rows, rows),
        check_vma=False,
    )
```

```python
import functools

import jax
import jax.numpy as jnp
from jax import lax
from jax.experimental import pallas as pl
from jax.experimental.pallas import tpu as pltpu
from jax.sharding import PartitionSpec as P

SUBSTEPS = 4
DAMPING = 0.05
EDGE = 8
F32 = jnp.float32
BF16 = jnp.bfloat16


def split3(x):
    hi = x.astype(BF16)
    rest = x - hi.astype(F32)
    mid = rest.astype(BF16)
    low = (rest - mid.astype(F32)).astype(BF16)
    return hi, mid, low


def dot(a, b, dims=((1,), (0,))):
    return lax.dot_general(a, b, (dims, ((), ())), preferred_element_type=F32)


def iota(shape, axis):
    return lax.broadcasted_iota(jnp.int32, shape, axis)


def kernel(
    n, per, wide,
    press, iterate, displace, velocity, stiffness, owners, diff_cur, step_cur, diff_past, step_past,
    new_ref, field_ref, speed_ref,
    vd, vs, masked, kbuf, halfmask, iter_v, own_v, ext, pext, cnt, raw, stage, pbuf, obuf, xbuf, gram, rsbuf, agbuf, prow, arbuf, elim, coefs,
    load_sem, small_sem, send_sem, recv_sem, halo_send, halo_recv,
):
    me = lax.axis_index("tile")
    left, right = lax.rem(me + n - 1, n), lax.rem(me + 1, n)
    lines = displace.shape[0]
    slots = iterate.shape[0]
    nc, npast = diff_cur.shape[0], diff_past.shape[0]
    cols = vd.shape[0]
    total = n * wide

    def peers(fn):
        def step(i, carry):
            fn(lax.rem(me + i, n))
            return carry

        lax.fori_loop(1, n, step, 0)

    barrier = pltpu.get_barrier_semaphore()
    peers(lambda p: pl.semaphore_signal(
        barrier, inc=1, device_id={"tile": p}, device_id_type=pl.DeviceIdType.MESH))

    loads = [
        pltpu.make_async_copy(diff_cur, vd.at[pl.ds(0, nc)], load_sem.at[0]),
        pltpu.make_async_copy(diff_past, vd.at[pl.ds(nc, npast)], load_sem.at[1]),
        pltpu.make_async_copy(step_cur, vs.at[pl.ds(0, nc)], load_sem.at[2]),
        pltpu.make_async_copy(step_past, vs.at[pl.ds(nc, npast)], load_sem.at[3]),
    ]
    small = [
        pltpu.make_async_copy(owners, own_v, small_sem.at[0]),
        pltpu.make_async_copy(displace, ext.at[0, pl.ds(EDGE, lines)], small_sem.at[1]),
        pltpu.make_async_copy(velocity, ext.at[1, pl.ds(EDGE, lines)], small_sem.at[2]),
        pltpu.make_async_copy(stiffness, ext.at[2, pl.ds(EDGE, lines)], small_sem.at[3]),
        pltpu.make_async_copy(iterate, iter_v, small_sem.at[4]),
    ]
    if wide != per:
        small.append(pltpu.make_async_copy(press, raw, small_sem.at[5]))
    else:
        small.append(pltpu.make_async_copy(
            press.at[pl.ds(pl.multiple_of(me * per, 8), per)], pbuf.at[me], small_sem.at[5]))
    for load in small + loads:
        load.start()

    def send(src, dst, phase, p):
        pltpu.make_async_remote_copy(
            src_ref=src, dst_ref=dst, send_sem=send_sem.at[phase], recv_sem=recv_sem.at[phase],
            device_id={"tile": p}, device_id_type=pl.DeviceIdType.MESH).start()

    def wait(buf, sem):
        part = buf.at[pl.ds(0, n - 1)]
        pltpu.make_async_copy(part, part, sem).wait()

    vd[nc + npast:cols] = jnp.zeros((cols - nc - npast, slots, 128), BF16)
    gram[...] = jnp.zeros_like(gram)
    kbuf[...] = jnp.zeros_like(kbuf)
    prow[...] = jnp.zeros_like(prow)
    small[0].wait()
    same = iota((lines, lines), 0) == iota((lines, lines), 1)
    own_row = jnp.broadcast_to(own_v[...].astype(F32), (lines, lines))
    own = jnp.sum(jnp.where(same, own_row, 0.0), axis=1, keepdims=True)
    lane_f = iota((lines, 128), 1).astype(F32)
    onehot = jnp.where(own == lane_f, 1.0, 0.0)
    cnt[me] = jnp.broadcast_to(jnp.sum(onehot, axis=0, keepdims=True), (8, 128))
    if wide != per:
        small[5].wait()
        stage[...] = jnp.zeros_like(stage)
        for s in range(n):
            stage[s, 0:per, :] = raw[s * per:(s + 1) * per, :]

    pl.semaphore_wait(barrier, n - 1)
    peers(lambda p: send(cnt.at[me], cnt.at[me], 0, p))

    def press_block(p):
        if wide != per:
            return stage.at[p]
        return press.at[pl.ds(pl.multiple_of(p * per, 8), per)]

    peers(lambda p: send(press_block(p), pbuf.at[me], 1, p))
    if wide != per:
        pbuf[me] = stage[me]

    def halos(buf, first, lead):
        moves = []
        for k, (src, dst, who) in enumerate((
            (EDGE, EDGE + lines, left),
            (lines, 0, right),
        )):
            moves.append(pltpu.make_async_remote_copy(
                src_ref=buf.at[lead + (pl.ds(src, EDGE),)], dst_ref=buf.at[lead + (pl.ds(dst, EDGE),)],
                send_sem=halo_send.at[first + k], recv_sem=halo_recv.at[first + k],
                device_id={"tile": who}, device_id_type=pl.DeviceIdType.MESH))
        for move in moves:
            move.start()
        return moves

    for load in small[1:4]:
        load.wait()
    field_halo = halos(ext, 0, (slice(None),))

    below = jnp.where(iota((lines, lines), 0) > iota((lines, lines), 1), 1.0, 0.0).astype(BF16)
    earlier = dot(below, onehot.astype(BF16))
    rank = jnp.sum(earlier * onehot, axis=1, keepdims=True)
    slot = own * float(wide) + rank
    chooser = jnp.where(slot == iota((lines, total), 1).astype(F32), 1.0, 0.0).astype(BF16)
    slot_row = jnp.sum(jnp.where(same, slot, 0.0), axis=0, keepdims=True)
    placer = jnp.where(slot_row == iota((total, lines), 0).astype(F32), 1.0, 0.0).astype(BF16)

    wait(cnt, recv_sem.at[0])
    mine = jnp.sum(jnp.where(iota((n, 8, 128), 2) == me, cnt[...], 0.0), axis=2, keepdims=True)
    mine = jnp.broadcast_to(mine, (n, 8, 128))
    if wide > 8:
        mine = jnp.concatenate([mine] * (wide // 8), axis=1)
    mask3 = jnp.where(iota((n, wide, 128), 1).astype(F32) < mine, 1.0, 0.0)

    def compact(cells):
        if wide == per:
            return cells.reshape(slots, 128)
        return jnp.concatenate([cells[s, 0:per, :] for s in range(n)], axis=0)

    mask = compact(mask3)
    halfmask[...] = mask.astype(BF16)

    loads[0].wait()
    loads[1].wait()

    def gather(a):
        return jnp.concatenate([
            vd[a * 16:(a + 1) * 16, r * 16:(r + 1) * 16, :].reshape(256, 128)
            for r in range(slots // 16)], axis=1)

    alike = (iota((256, 256), 0) & 15) == (iota((256, 256), 1) & 15)

    def gram_rows(a):
        for r in range(slots // 16):
            rows16 = slice(r * 16, (r + 1) * 16)
            block = vd[a * 16:(a + 1) * 16, rows16, :] * halfmask[rows16, :][None]
            masked[a % 2, :, r * 128:(r + 1) * 128] = block.reshape(256, 128)
        for b in range(a, cols // 16):
            prod = dot(masked[a % 2], gather(b), ((1,), (1,)))
            kept = jnp.sum(jnp.where(alike, prod, 0.0).reshape(16, 16, 256), axis=1)
            kbuf[a * 16:(a + 1) * 16, b * 256:(b + 1) * 256] = 0.5 * kept if a == b else kept

    gram_rows(0)

    wait(pbuf, recv_sem.at[1])
    if wide == per:
        small[5].wait()
    returned = pbuf[...].reshape(total, 128)
    hi, mid, low = split3(returned)
    pext[EDGE:EDGE + lines, :] = dot(chooser, hi) + dot(chooser, mid) + dot(chooser, low)
    press_halo = halos(pext, 2, ())

    gram_rows(1)

    for move in field_halo:
        move.wait()
    for move in press_halo:
        move.wait()
    w, v, stiff, force = ext[0], ext[1], ext[2], pext[...]
    rows = lines + 2 * EDGE
    lane = iota((rows, 128), 1)
    for _ in range(SUBSTEPS):
        upper = pltpu.roll(w, 1, 0)
        beneath = pltpu.roll(w, rows - 1, 0)
        lft = jnp.where(lane == 0, 0.0, pltpu.roll(w, 1, 1))
        rgt = jnp.where(lane == 127, 0.0, pltpu.roll(w, 127, 1))
        lapl = upper + beneath + (lft + rgt) - 4.0 * w
        v = v + (stiff * lapl + force - DAMPING * v)
        w = w + v
    field = w[EDGE:EDGE + lines, :]
    hi, mid, low = split3(field)
    placed = dot(placer, hi) + dot(placer, mid) + dot(placer, low)
    obuf[...] = placed.reshape(n, wide, 128)
    peers(lambda p: send(obuf.at[p], xbuf.at[me], 4, p))
    xbuf[me] = obuf[me]
    field_ref[...] = field
    speed_ref[...] = v[EDGE:EDGE + lines, :]

    for a in range(2, cols // 16):
        gram_rows(a)
    spread = jnp.where((iota((cols * 16, 128), 0) >> 4) == iota((cols * 16, 128), 1), 1.0, 0.0)
    spread = spread.astype(BF16)
    hi, mid, low = split3(kbuf[...])
    value = dot(hi, spread) + dot(mid, spread) + dot(low, spread)
    gram[0:cols // 8] = value.reshape(cols // 8, 8, 128)
    peers(lambda p: send(gram.at[p], rsbuf.at[me], 2, p))
    rsbuf[me] = gram[me]

    wait(xbuf, recv_sem.at[4])
    small[4].wait()
    x_tilde = compact(xbuf[...])
    resid = (mask * (x_tilde - iter_v[...])).astype(BF16).astype(F32)

    def product(k, carry):
        for u in range(10):
            prow[pl.ds(k * 10 + u, 1), :] = jnp.sum(
                vd[k * 10 + u].astype(F32) * resid, axis=0, keepdims=True)
        return carry

    steps = (nc + npast) // 10
    lax.fori_loop(0, steps // 2, product, 0)

    wait(rsbuf, recv_sem.at[2])
    agbuf[me] = jnp.sum(rsbuf[...], axis=0)
    peers(lambda p: send(agbuf.at[me], agbuf.at[me], 3, p))

    lax.fori_loop(steps // 2, steps, product, 0)
    ones = jnp.ones((8, 128), BF16)
    hi, mid, low = split3(prow[...])
    arbuf[me] = (dot(ones, hi, ((1,), (1,))) + dot(ones, mid, ((1,), (1,)))
                 + dot(ones, low, ((1,), (1,))))
    peers(lambda p: send(arbuf.at[me], arbuf.at[me], 5, p))

    wait(agbuf, recv_sem.at[3])
    half = agbuf[0:16].reshape(128, 128)
    full = half + half.T
    lane2, sub2 = iota((nc, 128), 1), iota((nc, 128), 0)
    unit = jnp.where(lane2 == sub2 + 64, 1.0, 0.0)
    cross = full[nc:2 * nc, :]
    past_part = jnp.where(lane2 < nc, pltpu.roll(cross, 128 - nc, 1), 0.0)
    elim[0] = jnp.where(lane2 < nc, full[0:nc, :], 0.0) + unit
    elim[1] = past_part + unit + jnp.where((lane2 == sub2) & (sub2 >= npast), 1.0, 0.0)
    lane3, sub3 = iota((2, nc, 128), 2), iota((2, nc, 128), 1)

    lane1 = iota((2, 1, 128), 2)

    def eliminate(i, carry):
        j = 2 * i
        now = elim[...]
        row0, row1 = elim[:, pl.ds(j, 1), :], elim[:, pl.ds(j + 1, 1), :]
        col0 = jnp.sum(jnp.where(lane3 == j, now, 0.0), axis=2, keepdims=True)
        col1 = jnp.sum(jnp.where(lane3 == j + 1, now, 0.0), axis=2, keepdims=True)
        top = jnp.sum(jnp.where(lane1 == j, row0, 0.0), axis=2, keepdims=True)
        side = jnp.sum(jnp.where(lane1 == j, row1, 0.0), axis=2, keepdims=True)
        corner = jnp.sum(jnp.where(lane1 == j + 1, row1, 0.0), axis=2, keepdims=True)
        factor = side / top
        row1 = row1 - factor * row0
        col1 = col1 - factor * col0
        corner = corner - factor * side
        later = now - col0 * (row0 / top) - col1 * (row1 / corner)
        elim[...] = jnp.where(sub3 > j + 1, later, jnp.where(sub3 == j + 1, row1, now))
        return carry

    lax.fori_loop(0, nc // 2, eliminate, 0)
    done = elim[...]
    diag2 = lane2 == sub2
    inverse, pivots = [], []
    for part in range(2):
        inverse.append(jnp.where(lane2 < nc, pltpu.roll(done[part], 64, 1), 0.0))
        pivots.append(jnp.sum(jnp.where(diag2, done[part], 0.0), axis=1, keepdims=True))

    loads[2].wait()
    loads[3].wait()
    wait(arbuf, recv_sem.at[5])
    rhs = jnp.sum(arbuf[...], axis=0)

    def solve(part, vector):
        inner = jnp.sum(inverse[part] * vector, axis=1, keepdims=True) / pivots[part]
        return jnp.sum(inverse[part] * inner, axis=0, keepdims=True)

    coeff = -solve(0, rhs[0:1, :])
    carried = jnp.sum(cross * coeff, axis=1, keepdims=True)
    carried = jnp.sum(jnp.where(diag2, carried, 0.0), axis=0, keepdims=True)
    past = solve(1, pltpu.roll(rhs, 128 - nc, 1)[0:1, :] + carried)
    for part, vector in enumerate((coeff, -past)):
        column = jnp.sum(jnp.where(diag2, vector, 0.0), axis=1, keepdims=True)
        coefs[part * nc:(part + 1) * nc, :] = jnp.broadcast_to(
            column, (nc, 128)).astype(BF16).astype(F32)

    def accumulate(k, acc):
        for u in range(10):
            acc = acc + coefs[pl.ds(k * 10 + u, 1), :] * vs[k * 10 + u].astype(F32)
        return acc

    update = lax.fori_loop(0, (nc + npast) // 10, accumulate, jnp.zeros((slots, 128), F32))
    new_ref[...] = mask * (x_tilde + update)

    for phase, buf in enumerate((cnt, pbuf, rsbuf, agbuf, xbuf, arbuf)):
        wait(buf, send_sem.at[phase])


def hand_over(a, b, c, a_out, b_out, c_out, a_held, b_held, c_held, sems):
    pairs = ((a, a_held, a_out), (b, b_held, b_out), (c, c_held, c_out))
    fetch = [pltpu.make_async_copy(src, held, sems.at[0, i]) for i, (src, held, _) in enumerate(pairs)]
    store = [pltpu.make_async_copy(held, dst, sems.at[1, i]) for i, (_, held, dst) in enumerate(pairs)]
    for move in fetch:
        move.start()
    for move, after in zip(fetch, store):
        move.wait()
        after.start()
    for move in store:
        move.wait()


def local(press, iterate, displace, velocity, stiffness, owners, diff_cur, step_cur, diff_past, step_past):
    n = lax.axis_size("tile")
    lines, slots = displace.shape[0], iterate.shape[0]
    per = slots // n
    wide = max(8, per)
    nc, npast = diff_cur.shape[0], diff_past.shape[0]
    cols = -(-2 * nc // 16) * 16
    vmem = pl.BlockSpec(memory_space=pltpu.VMEM)
    hbm = pl.BlockSpec(memory_space=pl.ANY)
    tiles = pltpu.VMEM((n, 8, 128), F32)
    blocks = pltpu.VMEM((n, wide, 128), F32)
    outs = pl.pallas_call(
        functools.partial(kernel, n, per, wide),
        out_shape=(
            jax.ShapeDtypeStruct((slots, 128), F32),
            jax.ShapeDtypeStruct((lines, 128), F32),
            jax.ShapeDtypeStruct((lines, 128), F32),
        ),
        in_specs=[hbm] * 10,
        out_specs=(vmem, vmem, vmem),
        scratch_shapes=[
            pltpu.VMEM((cols, slots, 128), BF16),
            pltpu.VMEM((nc + npast, slots, 128), BF16),
            pltpu.VMEM((2, 256, slots // 16 * 128), BF16),
            pltpu.VMEM((cols, cols * 16), F32),
            pltpu.VMEM((slots, 128), BF16),
            pltpu.VMEM((slots, 128), F32),
            pltpu.VMEM((1, lines), jnp.int32),
            pltpu.VMEM((3, lines + 2 * EDGE, 128), F32),
            pltpu.VMEM((lines + 2 * EDGE, 128), F32),
            tiles,
            pltpu.VMEM((slots if wide != per else 8, 128), F32),
            blocks if wide != per else pltpu.VMEM((8, 128), F32),
            blocks, blocks, blocks,
            tiles, tiles, tiles,
            pltpu.VMEM((128, 128), F32),
            tiles,
            pltpu.VMEM((2, nc, 128), F32),
            pltpu.VMEM((2 * nc, 128), F32),
            pltpu.SemaphoreType.DMA((4,)),
            pltpu.SemaphoreType.DMA((6,)),
            pltpu.SemaphoreType.DMA((6,)),
            pltpu.SemaphoreType.DMA((6,)),
            pltpu.SemaphoreType.DMA((4,)),
            pltpu.SemaphoreType.DMA((4,)),
        ],
        compiler_params=pltpu.CompilerParams(
            collective_id=0, has_side_effects=True, vmem_limit_bytes=62 * 1024 * 1024),
    )(press, iterate, displace, velocity, stiffness, owners.reshape(1, lines),
      diff_cur, step_cur, diff_past, step_past)
    return pl.pallas_call(
        hand_over,
        out_shape=tuple(jax.ShapeDtypeStruct(out.shape, out.dtype) for out in outs),
        in_specs=[hbm] * 3,
        out_specs=(hbm,) * 3,
        scratch_shapes=[pltpu.VMEM(out.shape, out.dtype) for out in outs]
        + [pltpu.SemaphoreType.DMA((2, 3))],
        compiler_params=pltpu.CompilerParams(vmem_limit_bytes=62 * 1024 * 1024),
    )(*outs)


def solution(mesh):
    rows = P(("runs", "tile"), None)
    deep = P(None, ("runs", "tile"), None)
    return jax.shard_map(
        local,
        mesh=mesh,
        in_specs=(rows,) * 6 + (deep,) * 4,
        out_specs=(rows, rows, rows),
        check_vma=False,
    )
```

```python
import functools

import jax
import jax.numpy as jnp
from jax import lax
from jax.experimental import pallas as pl
from jax.experimental.pallas import tpu as pltpu
from jax.sharding import PartitionSpec as P

SUBSTEPS = 4
DAMPING = 0.05
EDGE = 8
F32 = jnp.float32
BF16 = jnp.bfloat16


def split3(x):
    hi = x.astype(BF16)
    rest = x - hi.astype(F32)
    mid = rest.astype(BF16)
    low = (rest - mid.astype(F32)).astype(BF16)
    return hi, mid, low


def dot(a, b, dims=((1,), (0,))):
    return lax.dot_general(a, b, (dims, ((), ())), preferred_element_type=F32)


def iota(shape, axis):
    return lax.broadcasted_iota(jnp.int32, shape, axis)


def kernel(
    n, per, wide,
    press, iterate, displace, velocity, stiffness, owners, diff_cur, step_cur, diff_past, step_past,
    new_ref, field_ref, speed_ref,
    vd, vs, masked, kbuf, halfmask, iter_v, own_v, ext, pext, cnt, raw, stage, pbuf, obuf, xbuf, gram, rsbuf, agbuf, prow, arbuf, elim, coefs,
    load_sem, small_sem, send_sem, recv_sem, halo_send, halo_recv,
):
    me = lax.axis_index("tile")
    left, right = lax.rem(me + n - 1, n), lax.rem(me + 1, n)
    lines = displace.shape[0]
    slots = iterate.shape[0]
    nc, npast = diff_cur.shape[0], diff_past.shape[0]
    cols = vd.shape[0]
    total = n * wide

    def peers(fn):
        group = next(g for g in (5, 3, 1) if (n - 1) % g == 0)

        def step(i, carry):
            for u in range(group):
                fn(lax.rem(me + (i * group + u + 1), n))
            return carry

        lax.fori_loop(0, (n - 1) // group, step, 0)

    barrier = pltpu.get_barrier_semaphore()
    peers(lambda p: pl.semaphore_signal(
        barrier, inc=1, device_id={"tile": p}, device_id_type=pl.DeviceIdType.MESH))

    loads = [
        pltpu.make_async_copy(diff_cur, vd.at[pl.ds(0, nc)], load_sem.at[0]),
        pltpu.make_async_copy(diff_past, vd.at[pl.ds(nc, npast)], load_sem.at[1]),
        pltpu.make_async_copy(step_cur, vs.at[pl.ds(0, nc)], load_sem.at[2]),
        pltpu.make_async_copy(step_past, vs.at[pl.ds(nc, npast)], load_sem.at[3]),
    ]
    small = [
        pltpu.make_async_copy(owners, own_v, small_sem.at[0]),
        pltpu.make_async_copy(displace, ext.at[0, pl.ds(EDGE, lines)], small_sem.at[1]),
        pltpu.make_async_copy(velocity, ext.at[1, pl.ds(EDGE, lines)], small_sem.at[2]),
        pltpu.make_async_copy(stiffness, ext.at[2, pl.ds(EDGE, lines)], small_sem.at[3]),
        pltpu.make_async_copy(iterate, iter_v, small_sem.at[4]),
    ]
    if wide != per:
        small.append(pltpu.make_async_copy(press, raw, small_sem.at[5]))
    else:
        small.append(pltpu.make_async_copy(
            press.at[pl.ds(pl.multiple_of(me * per, 8), per)], pbuf.at[me], small_sem.at[5]))
    for load in small + loads:
        load.start()

    def send(src, dst, phase, p):
        pltpu.make_async_remote_copy(
            src_ref=src, dst_ref=dst, send_sem=send_sem.at[phase], recv_sem=recv_sem.at[phase],
            device_id={"tile": p}, device_id_type=pl.DeviceIdType.MESH).start()

    def wait(buf, sem):
        part = buf.at[pl.ds(0, n - 1)]
        pltpu.make_async_copy(part, part, sem).wait()

    vd[nc + npast:cols] = jnp.zeros((cols - nc - npast, slots, 128), BF16)
    gram[...] = jnp.zeros_like(gram)
    kbuf[...] = jnp.zeros_like(kbuf)
    prow[...] = jnp.zeros_like(prow)
    small[0].wait()
    same = iota((lines, lines), 0) == iota((lines, lines), 1)
    own_row = jnp.broadcast_to(own_v[...].astype(F32), (lines, lines))
    own = jnp.sum(jnp.where(same, own_row, 0.0), axis=1, keepdims=True)
    lane_f = iota((lines, 128), 1).astype(F32)
    onehot = jnp.where(own == lane_f, 1.0, 0.0)
    cnt[me] = jnp.broadcast_to(jnp.sum(onehot, axis=0, keepdims=True), (8, 128))
    if wide != per:
        small[5].wait()
        stage[...] = jnp.zeros_like(stage)
        for s in range(n):
            stage[s, 0:per, :] = raw[s * per:(s + 1) * per, :]

    pl.semaphore_wait(barrier, n - 1)
    peers(lambda p: send(cnt.at[me], cnt.at[me], 0, p))

    def press_block(p):
        if wide != per:
            return stage.at[p]
        return press.at[pl.ds(pl.multiple_of(p * per, 8), per)]

    peers(lambda p: send(press_block(p), pbuf.at[me], 1, p))
    if wide != per:
        pbuf[me] = stage[me]

    def halos(buf, first, lead):
        moves = []
        for k, (src, dst, who) in enumerate((
            (EDGE, EDGE + lines, left),
            (lines, 0, right),
        )):
            moves.append(pltpu.make_async_remote_copy(
                src_ref=buf.at[lead + (pl.ds(src, EDGE),)], dst_ref=buf.at[lead + (pl.ds(dst, EDGE),)],
                send_sem=halo_send.at[first + k], recv_sem=halo_recv.at[first + k],
                device_id={"tile": who}, device_id_type=pl.DeviceIdType.MESH))
        for move in moves:
            move.start()
        return moves

    for load in small[1:4]:
        load.wait()
    field_halo = halos(ext, 0, (slice(None),))

    below = jnp.where(iota((lines, lines), 0) > iota((lines, lines), 1), 1.0, 0.0).astype(BF16)
    earlier = dot(below, onehot.astype(BF16))
    rank = jnp.sum(earlier * onehot, axis=1, keepdims=True)
    slot = own * float(wide) + rank
    chooser = jnp.where(slot == iota((lines, total), 1).astype(F32), 1.0, 0.0).astype(BF16)
    slot_row = jnp.sum(jnp.where(same, slot, 0.0), axis=0, keepdims=True)
    placer = jnp.where(slot_row == iota((total, lines), 0).astype(F32), 1.0, 0.0).astype(BF16)

    wait(cnt, recv_sem.at[0])
    mine = jnp.sum(jnp.where(iota((n, 8, 128), 2) == me, cnt[...], 0.0), axis=2, keepdims=True)
    mine = jnp.broadcast_to(mine, (n, 8, 128))
    if wide > 8:
        mine = jnp.concatenate([mine] * (wide // 8), axis=1)
    mask3 = jnp.where(iota((n, wide, 128), 1).astype(F32) < mine, 1.0, 0.0)

    def compact(cells):
        if wide == per:
            return cells.reshape(slots, 128)
        return jnp.concatenate([cells[s, 0:per, :] for s in range(n)], axis=0)

    mask = compact(mask3)
    halfmask[...] = mask.astype(BF16)

    loads[0].wait()
    loads[1].wait()

    def gather(a):
        return jnp.concatenate([
            vd[a * 16:(a + 1) * 16, r * 16:(r + 1) * 16, :].reshape(256, 128)
            for r in range(slots // 16)], axis=1)

    alike = (iota((256, 256), 0) & 15) == (iota((256, 256), 1) & 15)

    def gram_rows(a):
        for r in range(slots // 16):
            rows16 = slice(r * 16, (r + 1) * 16)
            block = vd[a * 16:(a + 1) * 16, rows16, :] * halfmask[rows16, :][None]
            masked[a % 2, :, r * 128:(r + 1) * 128] = block.reshape(256, 128)
        for b in range(a, cols // 16):
            prod = dot(masked[a % 2], gather(b), ((1,), (1,)))
            kept = jnp.sum(jnp.where(alike, prod, 0.0).reshape(16, 16, 256), axis=1)
            kbuf[a * 16:(a + 1) * 16, b * 256:(b + 1) * 256] = 0.5 * kept if a == b else kept

    gram_rows(0)

    wait(pbuf, recv_sem.at[1])
    if wide == per:
        small[5].wait()
    returned = pbuf[...].reshape(total, 128)
    hi, mid, low = split3(returned)
    pext[EDGE:EDGE + lines, :] = dot(chooser, hi) + dot(chooser, mid) + dot(chooser, low)
    press_halo = halos(pext, 2, ())

    gram_rows(1)

    for move in field_halo:
        move.wait()
    for move in press_halo:
        move.wait()
    w, v, stiff, force = ext[0], ext[1], ext[2], pext[...]
    rows = lines + 2 * EDGE
    lane = iota((rows, 128), 1)
    for _ in range(SUBSTEPS):
        upper = pltpu.roll(w, 1, 0)
        beneath = pltpu.roll(w, rows - 1, 0)
        lft = jnp.where(lane == 0, 0.0, pltpu.roll(w, 1, 1))
        rgt = jnp.where(lane == 127, 0.0, pltpu.roll(w, 127, 1))
        lapl = upper + beneath + (lft + rgt) - 4.0 * w
        v = v + (stiff * lapl + force - DAMPING * v)
        w = w + v
    field = w[EDGE:EDGE + lines, :]
    hi, mid, low = split3(field)
    placed = dot(placer, hi) + dot(placer, mid) + dot(placer, low)
    obuf[...] = placed.reshape(n, wide, 128)
    peers(lambda p: send(obuf.at[p], xbuf.at[me], 4, p))
    xbuf[me] = obuf[me]
    field_ref[...] = field
    speed_ref[...] = v[EDGE:EDGE + lines, :]

    for a in range(2, cols // 16):
        gram_rows(a)
    spread = jnp.where((iota((cols * 16, 128), 0) >> 4) == iota((cols * 16, 128), 1), 1.0, 0.0)
    spread = spread.astype(BF16)
    hi, mid, low = split3(kbuf[...])
    value = dot(hi, spread) + dot(mid, spread) + dot(low, spread)
    gram[0:cols // 8] = value.reshape(cols // 8, 8, 128)
    peers(lambda p: send(gram.at[p], rsbuf.at[me], 2, p))
    rsbuf[me] = gram[me]

    wait(xbuf, recv_sem.at[4])
    small[4].wait()
    x_tilde = compact(xbuf[...])
    resid = (mask * (x_tilde - iter_v[...])).astype(BF16).astype(F32)

    def product(k, carry):
        for u in range(10):
            prow[pl.ds(k * 10 + u, 1), :] = jnp.sum(
                vd[k * 10 + u].astype(F32) * resid, axis=0, keepdims=True)
        return carry

    steps = (nc + npast) // 10
    lax.fori_loop(0, steps // 2, product, 0)

    wait(rsbuf, recv_sem.at[2])
    agbuf[me] = jnp.sum(rsbuf[...], axis=0)
    peers(lambda p: send(agbuf.at[me], agbuf.at[me], 3, p))

    lax.fori_loop(steps // 2, steps, product, 0)
    ones = jnp.ones((8, 128), BF16)
    hi, mid, low = split3(prow[...])
    arbuf[me] = (dot(ones, hi, ((1,), (1,))) + dot(ones, mid, ((1,), (1,)))
                 + dot(ones, low, ((1,), (1,))))
    peers(lambda p: send(arbuf.at[me], arbuf.at[me], 5, p))

    wait(agbuf, recv_sem.at[3])
    half = agbuf[0:16].reshape(128, 128)
    full = half + half.T
    lane2, sub2 = iota((nc, 128), 1), iota((nc, 128), 0)
    unit = jnp.where(lane2 == sub2 + 64, 1.0, 0.0)
    cross = full[nc:2 * nc, :]
    past_part = jnp.where(lane2 < nc, pltpu.roll(cross, 128 - nc, 1), 0.0)
    elim[0] = jnp.where(lane2 < nc, full[0:nc, :], 0.0) + unit
    elim[1] = past_part + unit + jnp.where((lane2 == sub2) & (sub2 >= npast), 1.0, 0.0)
    lane3, sub3 = iota((2, nc, 128), 2), iota((2, nc, 128), 1)

    lane1 = iota((2, 1, 128), 2)

    width = next(g for g in (4, 2, 1) if nc % g == 0)

    def lane_of(cells, lanes, j):
        return jnp.sum(jnp.where(lanes == j, cells, 0.0), axis=2, keepdims=True)

    def eliminate(i, carry):
        j = width * i
        now = elim[...]
        rows = [elim[:, pl.ds(j + u, 1), :] for u in range(width)]
        columns = [lane_of(now, lane3, j + u) for u in range(width)]
        entry = [[lane_of(rows[u], lane1, j + m) for m in range(u + 1)] for u in range(width)]
        for m in range(width):
            for u in range(m + 1, width):
                factor = entry[u][m] / entry[m][m]
                rows[u] = rows[u] - factor * rows[m]
                columns[u] = columns[u] - factor * columns[m]
                for k in range(m + 1, u + 1):
                    entry[u][k] = entry[u][k] - factor * entry[k][m]
        later = now
        for u in range(width):
            later = later - columns[u] * (rows[u] / entry[u][u])
        result = jnp.where(sub3 >= j + width, later, now)
        for u in range(1, width):
            result = jnp.where(sub3 == j + u, rows[u], result)
        elim[...] = result
        return carry

    lax.fori_loop(0, nc // width, eliminate, 0)
    done = elim[...]
    diag2 = lane2 == sub2
    inverse, pivots = [], []
    for part in range(2):
        inverse.append(jnp.where(lane2 < nc, pltpu.roll(done[part], 64, 1), 0.0))
        pivots.append(jnp.sum(jnp.where(diag2, done[part], 0.0), axis=1, keepdims=True))

    loads[2].wait()
    loads[3].wait()
    wait(arbuf, recv_sem.at[5])
    rhs = jnp.sum(arbuf[...], axis=0)

    def solve(part, vector):
        inner = jnp.sum(inverse[part] * vector, axis=1, keepdims=True) / pivots[part]
        return jnp.sum(inverse[part] * inner, axis=0, keepdims=True)

    coeff = -solve(0, rhs[0:1, :])
    carried = jnp.sum(cross * coeff, axis=1, keepdims=True)
    carried = jnp.sum(jnp.where(diag2, carried, 0.0), axis=0, keepdims=True)
    past = solve(1, pltpu.roll(rhs, 128 - nc, 1)[0:1, :] + carried)
    for part, vector in enumerate((coeff, -past)):
        column = jnp.sum(jnp.where(diag2, vector, 0.0), axis=1, keepdims=True)
        coefs[part * nc:(part + 1) * nc, :] = jnp.broadcast_to(
            column, (nc, 128)).astype(BF16).astype(F32)

    def accumulate(k, acc):
        for u in range(10):
            acc = acc + coefs[pl.ds(k * 10 + u, 1), :] * vs[k * 10 + u].astype(F32)
        return acc

    update = lax.fori_loop(0, (nc + npast) // 10, accumulate, jnp.zeros((slots, 128), F32))
    new_ref[...] = mask * (x_tilde + update)

    for phase, buf in enumerate((cnt, pbuf, rsbuf, agbuf, xbuf, arbuf)):
        wait(buf, send_sem.at[phase])


def hand_over(a, b, c, a_out, b_out, c_out, a_held, b_held, c_held, sems):
    pairs = ((a, a_held, a_out), (b, b_held, b_out), (c, c_held, c_out))
    fetch = [pltpu.make_async_copy(src, held, sems.at[0, i]) for i, (src, held, _) in enumerate(pairs)]
    store = [pltpu.make_async_copy(held, dst, sems.at[1, i]) for i, (_, held, dst) in enumerate(pairs)]
    for move in fetch:
        move.start()
    for move, after in zip(fetch, store):
        move.wait()
        after.start()
    for move in store:
        move.wait()


def local(press, iterate, displace, velocity, stiffness, owners, diff_cur, step_cur, diff_past, step_past):
    n = lax.axis_size("tile")
    lines, slots = displace.shape[0], iterate.shape[0]
    per = slots // n
    wide = max(8, per)
    nc, npast = diff_cur.shape[0], diff_past.shape[0]
    cols = -(-2 * nc // 16) * 16
    vmem = pl.BlockSpec(memory_space=pltpu.VMEM)
    hbm = pl.BlockSpec(memory_space=pl.ANY)
    tiles = pltpu.VMEM((n, 8, 128), F32)
    blocks = pltpu.VMEM((n, wide, 128), F32)
    outs = pl.pallas_call(
        functools.partial(kernel, n, per, wide),
        out_shape=(
            jax.ShapeDtypeStruct((slots, 128), F32),
            jax.ShapeDtypeStruct((lines, 128), F32),
            jax.ShapeDtypeStruct((lines, 128), F32),
        ),
        in_specs=[hbm] * 10,
        out_specs=(vmem, vmem, vmem),
        scratch_shapes=[
            pltpu.VMEM((cols, slots, 128), BF16),
            pltpu.VMEM((nc + npast, slots, 128), BF16),
            pltpu.VMEM((2, 256, slots // 16 * 128), BF16),
            pltpu.VMEM((cols, cols * 16), F32),
            pltpu.VMEM((slots, 128), BF16),
            pltpu.VMEM((slots, 128), F32),
            pltpu.VMEM((1, lines), jnp.int32),
            pltpu.VMEM((3, lines + 2 * EDGE, 128), F32),
            pltpu.VMEM((lines + 2 * EDGE, 128), F32),
            tiles,
            pltpu.VMEM((slots if wide != per else 8, 128), F32),
            blocks if wide != per else pltpu.VMEM((8, 128), F32),
            blocks, blocks, blocks,
            tiles, tiles, tiles,
            pltpu.VMEM((128, 128), F32),
            tiles,
            pltpu.VMEM((2, nc, 128), F32),
            pltpu.VMEM((2 * nc, 128), F32),
            pltpu.SemaphoreType.DMA((4,)),
            pltpu.SemaphoreType.DMA((6,)),
            pltpu.SemaphoreType.DMA((6,)),
            pltpu.SemaphoreType.DMA((6,)),
            pltpu.SemaphoreType.DMA((4,)),
            pltpu.SemaphoreType.DMA((4,)),
        ],
        compiler_params=pltpu.CompilerParams(
            collective_id=0, has_side_effects=True, vmem_limit_bytes=62 * 1024 * 1024),
    )(press, iterate, displace, velocity, stiffness, owners.reshape(1, lines),
      diff_cur, step_cur, diff_past, step_past)
    return pl.pallas_call(
        hand_over,
        out_shape=tuple(jax.ShapeDtypeStruct(out.shape, out.dtype) for out in outs),
        in_specs=[hbm] * 3,
        out_specs=(hbm,) * 3,
        scratch_shapes=[pltpu.VMEM(out.shape, out.dtype) for out in outs]
        + [pltpu.SemaphoreType.DMA((2, 3))],
        compiler_params=pltpu.CompilerParams(vmem_limit_bytes=62 * 1024 * 1024),
    )(*outs)


def solution(mesh):
    rows = P(("runs", "tile"), None)
    deep = P(None, ("runs", "tile"), None)
    return jax.shard_map(
        local,
        mesh=mesh,
        in_specs=(rows,) * 6 + (deep,) * 4,
        out_specs=(rows, rows, rows),
        check_vma=False,
    )
```

```python
import functools

import jax
import jax.numpy as jnp
from jax import lax
from jax.experimental import pallas as pl
from jax.experimental.pallas import tpu as pltpu
from jax.sharding import PartitionSpec as P

SUBSTEPS = 4
DAMPING = 0.05
EDGE = 8
F32 = jnp.float32
BF16 = jnp.bfloat16


def split3(x):
    hi = x.astype(BF16)
    rest = x - hi.astype(F32)
    mid = rest.astype(BF16)
    low = (rest - mid.astype(F32)).astype(BF16)
    return hi, mid, low


def dot(a, b, dims=((1,), (0,))):
    return lax.dot_general(a, b, (dims, ((), ())), preferred_element_type=F32)


def iota(shape, axis):
    return lax.broadcasted_iota(jnp.int32, shape, axis)


def kernel(
    n, per, wide,
    press, iterate, displace, velocity, stiffness, owners, diff_cur, step_cur, diff_past, step_past,
    new_ref, field_ref, speed_ref,
    vd, vs, masked, kbuf, halfmask, iter_v, own_v, ext, pext, cnt, raw, stage, pbuf, obuf, xbuf, gram, rsbuf, agbuf, prow, arbuf, elim, coefs,
    load_sem, small_sem, send_sem, recv_sem, halo_send, halo_recv,
):
    me = lax.axis_index("tile")
    left, right = lax.rem(me + n - 1, n), lax.rem(me + 1, n)
    lines = displace.shape[0]
    slots = iterate.shape[0]
    nc, npast = diff_cur.shape[0], diff_past.shape[0]
    cols = kbuf.shape[0]
    total = n * wide

    def peers(fn):
        group = next(g for g in (5, 3, 1) if (n - 1) % g == 0)

        def step(i, carry):
            for u in range(group):
                fn(lax.rem(me + (i * group + u + 1), n))
            return carry

        lax.fori_loop(0, (n - 1) // group, step, 0)

    barrier = pltpu.get_barrier_semaphore()
    peers(lambda p: pl.semaphore_signal(
        barrier, inc=1, device_id={"tile": p}, device_id_type=pl.DeviceIdType.MESH))

    loads = [
        pltpu.make_async_copy(diff_cur, vd.at[pl.ds(0, nc)], load_sem.at[0]),
        pltpu.make_async_copy(diff_past, vd.at[pl.ds(nc, npast)], load_sem.at[1]),
        pltpu.make_async_copy(step_cur, vs.at[pl.ds(0, nc)], load_sem.at[2]),
        pltpu.make_async_copy(step_past, vs.at[pl.ds(nc, npast)], load_sem.at[3]),
    ]
    small = [
        pltpu.make_async_copy(owners, own_v, small_sem.at[0]),
        pltpu.make_async_copy(displace, ext.at[0, pl.ds(EDGE, lines)], small_sem.at[1]),
        pltpu.make_async_copy(velocity, ext.at[1, pl.ds(EDGE, lines)], small_sem.at[2]),
        pltpu.make_async_copy(stiffness, ext.at[2, pl.ds(EDGE, lines)], small_sem.at[3]),
        pltpu.make_async_copy(iterate, iter_v, small_sem.at[4]),
    ]
    if wide != per:
        small.append(pltpu.make_async_copy(press, raw, small_sem.at[5]))
    else:
        small.append(pltpu.make_async_copy(
            press.at[pl.ds(pl.multiple_of(me * per, 8), per)], pbuf.at[me], small_sem.at[5]))
    for load in small + loads:
        load.start()

    def send(src, dst, phase, p):
        pltpu.make_async_remote_copy(
            src_ref=src, dst_ref=dst, send_sem=send_sem.at[phase], recv_sem=recv_sem.at[phase],
            device_id={"tile": p}, device_id_type=pl.DeviceIdType.MESH).start()

    def wait(buf, sem):
        part = buf.at[pl.ds(0, n - 1)]
        pltpu.make_async_copy(part, part, sem).wait()

    vd[nc + npast:] = jnp.zeros((vd.shape[0] - nc - npast, slots, 128), BF16)
    gram[...] = jnp.zeros_like(gram)
    kbuf[...] = jnp.zeros_like(kbuf)
    prow[...] = jnp.zeros_like(prow)
    small[0].wait()
    same = iota((lines, lines), 0) == iota((lines, lines), 1)
    own_row = jnp.broadcast_to(own_v[...].astype(F32), (lines, lines))
    own = jnp.sum(jnp.where(same, own_row, 0.0), axis=1, keepdims=True)
    lane_f = iota((lines, 128), 1).astype(F32)
    onehot = jnp.where(own == lane_f, 1.0, 0.0)
    cnt[me] = jnp.broadcast_to(jnp.sum(onehot, axis=0, keepdims=True), (8, 128))
    if wide != per:
        small[5].wait()
        stage[...] = jnp.zeros_like(stage)
        for s in range(n):
            stage[s, 0:per, :] = raw[s * per:(s + 1) * per, :]

    pl.semaphore_wait(barrier, n - 1)
    peers(lambda p: send(cnt.at[me], cnt.at[me], 0, p))

    def press_block(p):
        if wide != per:
            return stage.at[p]
        return press.at[pl.ds(pl.multiple_of(p * per, 8), per)]

    peers(lambda p: send(press_block(p), pbuf.at[me], 1, p))
    if wide != per:
        pbuf[me] = stage[me]

    def halos(buf, first, lead):
        moves = []
        for k, (src, dst, who) in enumerate((
            (EDGE, EDGE + lines, left),
            (lines, 0, right),
        )):
            moves.append(pltpu.make_async_remote_copy(
                src_ref=buf.at[lead + (pl.ds(src, EDGE),)], dst_ref=buf.at[lead + (pl.ds(dst, EDGE),)],
                send_sem=halo_send.at[first + k], recv_sem=halo_recv.at[first + k],
                device_id={"tile": who}, device_id_type=pl.DeviceIdType.MESH))
        for move in moves:
            move.start()
        return moves

    for load in small[1:4]:
        load.wait()
    field_halo = halos(ext, 0, (slice(None),))

    below = jnp.where(iota((lines, lines), 0) > iota((lines, lines), 1), 1.0, 0.0).astype(BF16)
    earlier = dot(below, onehot.astype(BF16))
    rank = jnp.sum(earlier * onehot, axis=1, keepdims=True)
    slot = own * float(wide) + rank
    chooser = jnp.where(slot == iota((lines, total), 1).astype(F32), 1.0, 0.0).astype(BF16)
    slot_row = jnp.sum(jnp.where(same, slot, 0.0), axis=0, keepdims=True)
    placer = jnp.where(slot_row == iota((total, lines), 0).astype(F32), 1.0, 0.0).astype(BF16)

    wait(cnt, recv_sem.at[0])
    mine = jnp.sum(jnp.where(iota((n, 8, 128), 2) == me, cnt[...], 0.0), axis=2, keepdims=True)
    mine = jnp.broadcast_to(mine, (n, 8, 128))
    if wide > 8:
        mine = jnp.concatenate([mine] * (wide // 8), axis=1)
    mask3 = jnp.where(iota((n, wide, 128), 1).astype(F32) < mine, 1.0, 0.0)

    def compact(cells):
        if wide == per:
            return cells.reshape(slots, 128)
        return jnp.concatenate([cells[s, 0:per, :] for s in range(n)], axis=0)

    mask = compact(mask3)
    halfmask[...] = mask.astype(BF16)

    loads[0].wait()
    loads[1].wait()

    used = vd.shape[0]
    sizes = [min(16, used - a * 16) for a in range(cols // 16)]

    def gather(a):
        size = sizes[a]
        return jnp.concatenate([
            vd[a * 16:a * 16 + size, r * 16:(r + 1) * 16, :].reshape(size * 16, 128)
            for r in range(slots // 16)], axis=1)

    alike = (iota((256, 256), 0) & 15) == (iota((256, 256), 1) & 15)

    def gram_rows(a):
        size = sizes[a]
        for r in range(slots // 16):
            rows16 = slice(r * 16, (r + 1) * 16)
            block = vd[a * 16:a * 16 + size, rows16, :] * halfmask[rows16, :][None]
            masked[a % 2, 0:size * 16, r * 128:(r + 1) * 128] = block.reshape(size * 16, 128)
        for b in range(a, cols // 16):
            high, wide_b = size * 16, sizes[b] * 16
            prod = dot(masked[a % 2, 0:high, :], gather(b), ((1,), (1,)))
            kept = jnp.where(alike[0:high, 0:wide_b], prod, 0.0).reshape(size, 16, wide_b)
            kept = jnp.sum(kept, axis=1)
            kbuf[a * 16:a * 16 + size, b * 256:b * 256 + wide_b] = 0.5 * kept if a == b else kept

    gram_rows(0)

    wait(pbuf, recv_sem.at[1])
    if wide == per:
        small[5].wait()
    returned = pbuf[...].reshape(total, 128)
    hi, mid, low = split3(returned)
    pext[EDGE:EDGE + lines, :] = dot(chooser, hi) + dot(chooser, mid) + dot(chooser, low)
    press_halo = halos(pext, 2, ())

    gram_rows(1)

    for move in field_halo:
        move.wait()
    for move in press_halo:
        move.wait()
    w, v, stiff, force = ext[0], ext[1], ext[2], pext[...]
    rows = lines + 2 * EDGE
    lane = iota((rows, 128), 1)
    for _ in range(SUBSTEPS):
        upper = pltpu.roll(w, 1, 0)
        beneath = pltpu.roll(w, rows - 1, 0)
        lft = jnp.where(lane == 0, 0.0, pltpu.roll(w, 1, 1))
        rgt = jnp.where(lane == 127, 0.0, pltpu.roll(w, 127, 1))
        lapl = upper + beneath + (lft + rgt) - 4.0 * w
        v = v + (stiff * lapl + force - DAMPING * v)
        w = w + v
    field = w[EDGE:EDGE + lines, :]
    hi, mid, low = split3(field)
    placed = dot(placer, hi) + dot(placer, mid) + dot(placer, low)
    obuf[...] = placed.reshape(n, wide, 128)
    peers(lambda p: send(obuf.at[p], xbuf.at[me], 4, p))
    xbuf[me] = obuf[me]
    field_ref[...] = field
    speed_ref[...] = v[EDGE:EDGE + lines, :]

    for a in range(2, cols // 16):
        gram_rows(a)
    spread = jnp.where((iota((cols * 16, 128), 0) >> 4) == iota((cols * 16, 128), 1), 1.0, 0.0)
    spread = spread.astype(BF16)
    hi, mid, low = split3(kbuf[...])
    value = dot(hi, spread) + dot(mid, spread) + dot(low, spread)
    gram[0:cols // 8] = value.reshape(cols // 8, 8, 128)
    peers(lambda p: send(gram.at[p], rsbuf.at[me], 2, p))
    rsbuf[me] = gram[me]

    wait(xbuf, recv_sem.at[4])
    small[4].wait()
    x_tilde = compact(xbuf[...])
    resid = (mask * (x_tilde - iter_v[...])).astype(BF16).astype(F32)

    def product(k, carry):
        for u in range(10):
            prow[pl.ds(k * 10 + u, 1), :] = jnp.sum(
                vd[k * 10 + u].astype(F32) * resid, axis=0, keepdims=True)
        return carry

    steps = (nc + npast) // 10
    lax.fori_loop(0, steps // 2, product, 0)

    wait(rsbuf, recv_sem.at[2])
    agbuf[me] = jnp.sum(rsbuf[...], axis=0)
    peers(lambda p: send(agbuf.at[me], agbuf.at[me], 3, p))

    lax.fori_loop(steps // 2, steps, product, 0)
    ones = jnp.ones((8, 128), BF16)
    hi, mid, low = split3(prow[...])
    arbuf[me] = (dot(ones, hi, ((1,), (1,))) + dot(ones, mid, ((1,), (1,)))
                 + dot(ones, low, ((1,), (1,))))
    peers(lambda p: send(arbuf.at[me], arbuf.at[me], 5, p))

    wait(agbuf, recv_sem.at[3])
    half = agbuf[0:16].reshape(128, 128)
    full = half + half.T
    lane2, sub2 = iota((nc, 128), 1), iota((nc, 128), 0)
    unit = jnp.where(lane2 == sub2 + 64, 1.0, 0.0)
    cross = full[nc:2 * nc, :]
    past_part = jnp.where(lane2 < nc, pltpu.roll(cross, 128 - nc, 1), 0.0)
    elim[0] = jnp.where(lane2 < nc, full[0:nc, :], 0.0) + unit
    elim[1] = past_part + unit + jnp.where((lane2 == sub2) & (sub2 >= npast), 1.0, 0.0)
    lane3, sub3 = iota((2, nc, 128), 2), iota((2, nc, 128), 1)

    lane1 = iota((2, 1, 128), 2)

    width = next(g for g in (4, 2, 1) if nc % g == 0)

    def lane_of(cells, lanes, j):
        return jnp.sum(jnp.where(lanes == j, cells, 0.0), axis=2, keepdims=True)

    def eliminate(j, now):
        rows = [now[:, j + u:j + u + 1, :] for u in range(width)]
        columns = [lane_of(now, lane3, j + u) for u in range(width)]
        entry = [[lane_of(rows[u], lane1, j + m) for m in range(u + 1)] for u in range(width)]
        for m in range(width):
            for u in range(m + 1, width):
                factor = entry[u][m] / entry[m][m]
                rows[u] = rows[u] - factor * rows[m]
                columns[u] = columns[u] - factor * columns[m]
                for k in range(m + 1, u + 1):
                    entry[u][k] = entry[u][k] - factor * entry[k][m]
        later = now
        for u in range(width):
            later = later - columns[u] * (rows[u] / entry[u][u])
        result = jnp.where(sub3 >= j + width, later, now)
        for u in range(1, width):
            result = jnp.where(sub3 == j + u, rows[u], result)
        return result

    done = elim[...]
    for j in range(0, nc, width):
        done = eliminate(j, done)
    diag2 = lane2 == sub2
    inverse, pivots = [], []
    for part in range(2):
        inverse.append(jnp.where(lane2 < nc, pltpu.roll(done[part], 64, 1), 0.0))
        pivots.append(jnp.sum(jnp.where(diag2, done[part], 0.0), axis=1, keepdims=True))

    loads[2].wait()
    loads[3].wait()
    wait(arbuf, recv_sem.at[5])
    rhs = jnp.sum(arbuf[...], axis=0)

    def solve(part, vector):
        inner = jnp.sum(inverse[part] * vector, axis=1, keepdims=True) / pivots[part]
        return jnp.sum(inverse[part] * inner, axis=0, keepdims=True)

    coeff = -solve(0, rhs[0:1, :])
    carried = jnp.sum(cross * coeff, axis=1, keepdims=True)
    carried = jnp.sum(jnp.where(diag2, carried, 0.0), axis=0, keepdims=True)
    past = solve(1, pltpu.roll(rhs, 128 - nc, 1)[0:1, :] + carried)
    for part, vector in enumerate((coeff, -past)):
        column = jnp.sum(jnp.where(diag2, vector, 0.0), axis=1, keepdims=True)
        coefs[part * nc:(part + 1) * nc, :] = jnp.broadcast_to(
            column, (nc, 128)).astype(BF16).astype(F32)

    def accumulate(k, acc):
        for u in range(10):
            acc = acc + coefs[pl.ds(k * 10 + u, 1), :] * vs[k * 10 + u].astype(F32)
        return acc

    update = lax.fori_loop(0, (nc + npast) // 10, accumulate, jnp.zeros((slots, 128), F32))
    new_ref[...] = mask * (x_tilde + update)

    for phase, buf in enumerate((cnt, pbuf, rsbuf, agbuf, xbuf, arbuf)):
        wait(buf, send_sem.at[phase])


def hand_over(a, b, c, a_out, b_out, c_out, a_held, b_held, c_held, sems):
    pairs = ((a, a_held, a_out), (b, b_held, b_out), (c, c_held, c_out))
    fetch = [pltpu.make_async_copy(src, held, sems.at[0, i]) for i, (src, held, _) in enumerate(pairs)]
    store = [pltpu.make_async_copy(held, dst, sems.at[1, i]) for i, (_, held, dst) in enumerate(pairs)]
    for move in fetch:
        move.start()
    for move, after in zip(fetch, store):
        move.wait()
        after.start()
    for move in store:
        move.wait()


def local(press, iterate, displace, velocity, stiffness, owners, diff_cur, step_cur, diff_past, step_past):
    n = lax.axis_size("tile")
    lines, slots = displace.shape[0], iterate.shape[0]
    per = slots // n
    wide = max(8, per)
    nc, npast = diff_cur.shape[0], diff_past.shape[0]
    cols = -(-2 * nc // 16) * 16
    vmem = pl.BlockSpec(memory_space=pltpu.VMEM)
    hbm = pl.BlockSpec(memory_space=pl.ANY)
    tiles = pltpu.VMEM((n, 8, 128), F32)
    blocks = pltpu.VMEM((n, wide, 128), F32)
    outs = pl.pallas_call(
        functools.partial(kernel, n, per, wide),
        out_shape=(
            jax.ShapeDtypeStruct((slots, 128), F32),
            jax.ShapeDtypeStruct((lines, 128), F32),
            jax.ShapeDtypeStruct((lines, 128), F32),
        ),
        in_specs=[hbm] * 10,
        out_specs=(vmem, vmem, vmem),
        scratch_shapes=[
            pltpu.VMEM((-(-(nc + npast) // 8) * 8, slots, 128), BF16),
            pltpu.VMEM((nc + npast, slots, 128), BF16),
            pltpu.VMEM((2, 256, slots // 16 * 128), BF16),
            pltpu.VMEM((cols, cols * 16), F32),
            pltpu.VMEM((slots, 128), BF16),
            pltpu.VMEM((slots, 128), F32),
            pltpu.VMEM((1, lines), jnp.int32),
            pltpu.VMEM((3, lines + 2 * EDGE, 128), F32),
            pltpu.VMEM((lines + 2 * EDGE, 128), F32),
            tiles,
            pltpu.VMEM((slots if wide != per else 8, 128), F32),
            blocks if wide != per else pltpu.VMEM((8, 128), F32),
            blocks, blocks, blocks,
            tiles, tiles, tiles,
            pltpu.VMEM((128, 128), F32),
            tiles,
            pltpu.VMEM((2, nc, 128), F32),
            pltpu.VMEM((2 * nc, 128), F32),
            pltpu.SemaphoreType.DMA((4,)),
            pltpu.SemaphoreType.DMA((6,)),
            pltpu.SemaphoreType.DMA((6,)),
            pltpu.SemaphoreType.DMA((6,)),
            pltpu.SemaphoreType.DMA((4,)),
            pltpu.SemaphoreType.DMA((4,)),
        ],
        compiler_params=pltpu.CompilerParams(
            collective_id=0, has_side_effects=True, vmem_limit_bytes=62 * 1024 * 1024),
    )(press, iterate, displace, velocity, stiffness, owners.reshape(1, lines),
      diff_cur, step_cur, diff_past, step_past)
    return pl.pallas_call(
        hand_over,
        out_shape=tuple(jax.ShapeDtypeStruct(out.shape, out.dtype) for out in outs),
        in_specs=[hbm] * 3,
        out_specs=(hbm,) * 3,
        scratch_shapes=[pltpu.VMEM(out.shape, out.dtype) for out in outs]
        + [pltpu.SemaphoreType.DMA((2, 3))],
        compiler_params=pltpu.CompilerParams(vmem_limit_bytes=62 * 1024 * 1024),
    )(*outs)


def solution(mesh):
    rows = P(("runs", "tile"), None)
    deep = P(None, ("runs", "tile"), None)
    return jax.shard_map(
        local,
        mesh=mesh,
        in_specs=(rows,) * 6 + (deep,) * 4,
        out_specs=(rows, rows, rows),
        check_vma=False,
    )
```

```python
import functools

import jax
import jax.numpy as jnp
from jax import lax
from jax.experimental import pallas as pl
from jax.experimental.pallas import tpu as pltpu
from jax.sharding import PartitionSpec as P

SUBSTEPS = 4
DAMPING = 0.05
EDGE = 8
F32 = jnp.float32
BF16 = jnp.bfloat16


def split3(x):
    hi = x.astype(BF16)
    rest = x - hi.astype(F32)
    mid = rest.astype(BF16)
    low = (rest - mid.astype(F32)).astype(BF16)
    return hi, mid, low


def dot(a, b, dims=((1,), (0,))):
    return lax.dot_general(a, b, (dims, ((), ())), preferred_element_type=F32)


def iota(shape, axis):
    return lax.broadcasted_iota(jnp.int32, shape, axis)


def kernel(
    n, per, wide,
    press, iterate, displace, velocity, stiffness, owners, diff_cur, step_cur, diff_past, step_past,
    new_ref, field_ref, speed_ref,
    vd, vs, masked, kbuf, halfmask, iter_v, own_v, ext, pext, cnt, raw, stage, pbuf, obuf, xbuf, gram, rsbuf, agbuf, prow, arbuf, elim, coefs,
    load_sem, small_sem, send_sem, recv_sem, halo_send, halo_recv,
):
    me = lax.axis_index("tile")
    left, right = lax.rem(me + n - 1, n), lax.rem(me + 1, n)
    lines = displace.shape[0]
    slots = iterate.shape[0]
    nc, npast = diff_cur.shape[0], diff_past.shape[0]
    cols = kbuf.shape[0]
    total = n * wide

    def peers(fn):
        group = next(g for g in (5, 3, 1) if (n - 1) % g == 0)

        def step(i, carry):
            for u in range(group):
                fn(lax.rem(me + (i * group + u + 1), n))
            return carry

        lax.fori_loop(0, (n - 1) // group, step, 0)

    barrier = pltpu.get_barrier_semaphore()
    peers(lambda p: pl.semaphore_signal(
        barrier, inc=1, device_id={"tile": p}, device_id_type=pl.DeviceIdType.MESH))

    loads = [
        pltpu.make_async_copy(diff_cur, vd.at[pl.ds(0, nc)], load_sem.at[0]),
        pltpu.make_async_copy(diff_past, vd.at[pl.ds(nc, npast)], load_sem.at[1]),
        pltpu.make_async_copy(step_cur, vs.at[pl.ds(0, nc)], load_sem.at[2]),
        pltpu.make_async_copy(step_past, vs.at[pl.ds(nc, npast)], load_sem.at[3]),
    ]
    small = [
        pltpu.make_async_copy(owners, own_v, small_sem.at[0]),
        pltpu.make_async_copy(displace, ext.at[0, pl.ds(EDGE, lines)], small_sem.at[1]),
        pltpu.make_async_copy(velocity, ext.at[1, pl.ds(EDGE, lines)], small_sem.at[2]),
        pltpu.make_async_copy(stiffness, ext.at[2, pl.ds(EDGE, lines)], small_sem.at[3]),
        pltpu.make_async_copy(iterate, iter_v, small_sem.at[4]),
    ]
    if wide != per:
        small.append(pltpu.make_async_copy(press, raw, small_sem.at[5]))
    else:
        small.append(pltpu.make_async_copy(
            press.at[pl.ds(pl.multiple_of(me * per, 8), per)], pbuf.at[me], small_sem.at[5]))
    for load in small + loads:
        load.start()

    def send(src, dst, phase, p):
        pltpu.make_async_remote_copy(
            src_ref=src, dst_ref=dst, send_sem=send_sem.at[phase], recv_sem=recv_sem.at[phase],
            device_id={"tile": p}, device_id_type=pl.DeviceIdType.MESH).start()

    def wait(buf, sem):
        part = buf.at[pl.ds(0, n - 1)]
        pltpu.make_async_copy(part, part, sem).wait()

    vd[nc + npast:] = jnp.zeros((vd.shape[0] - nc - npast, slots, 128), BF16)
    gram[...] = jnp.zeros_like(gram)
    kbuf[...] = jnp.zeros_like(kbuf)
    prow[...] = jnp.zeros_like(prow)
    small[0].wait()
    same = iota((lines, lines), 0) == iota((lines, lines), 1)
    own_row = jnp.broadcast_to(own_v[...].astype(F32), (lines, lines))
    own = jnp.sum(jnp.where(same, own_row, 0.0), axis=1, keepdims=True)
    lane_f = iota((lines, 128), 1).astype(F32)
    onehot = jnp.where(own == lane_f, 1.0, 0.0)
    cnt[me] = jnp.broadcast_to(jnp.sum(onehot, axis=0, keepdims=True), (8, 128))
    if wide != per:
        small[5].wait()
        stage[...] = jnp.zeros_like(stage)
        for s in range(n):
            stage[s, 0:per, :] = raw[s * per:(s + 1) * per, :]

    pl.semaphore_wait(barrier, n - 1)
    peers(lambda p: send(cnt.at[me], cnt.at[me], 0, p))

    def press_block(p):
        if wide != per:
            return stage.at[p]
        return press.at[pl.ds(pl.multiple_of(p * per, 8), per)]

    peers(lambda p: send(press_block(p), pbuf.at[me], 1, p))
    if wide != per:
        pbuf[me] = stage[me]

    def halos(buf, first, lead):
        moves = []
        for k, (src, dst, who) in enumerate((
            (EDGE, EDGE + lines, left),
            (lines, 0, right),
        )):
            moves.append(pltpu.make_async_remote_copy(
                src_ref=buf.at[lead + (pl.ds(src, EDGE),)], dst_ref=buf.at[lead + (pl.ds(dst, EDGE),)],
                send_sem=halo_send.at[first + k], recv_sem=halo_recv.at[first + k],
                device_id={"tile": who}, device_id_type=pl.DeviceIdType.MESH))
        for move in moves:
            move.start()
        return moves

    for load in small[1:4]:
        load.wait()
    field_halo = halos(ext, 0, (slice(None),))

    below = jnp.where(iota((lines, lines), 0) > iota((lines, lines), 1), 1.0, 0.0).astype(BF16)
    earlier = dot(below, onehot.astype(BF16))
    rank = jnp.sum(earlier * onehot, axis=1, keepdims=True)
    slot = own * float(wide) + rank
    chooser = jnp.where(slot == iota((lines, total), 1).astype(F32), 1.0, 0.0).astype(BF16)
    slot_row = jnp.sum(jnp.where(same, slot, 0.0), axis=0, keepdims=True)
    placer = jnp.where(slot_row == iota((total, lines), 0).astype(F32), 1.0, 0.0).astype(BF16)

    wait(cnt, recv_sem.at[0])
    mine = jnp.sum(jnp.where(iota((n, 8, 128), 2) == me, cnt[...], 0.0), axis=2, keepdims=True)
    mine = jnp.broadcast_to(mine, (n, 8, 128))
    if wide > 8:
        mine = jnp.concatenate([mine] * (wide // 8), axis=1)
    mask3 = jnp.where(iota((n, wide, 128), 1).astype(F32) < mine, 1.0, 0.0)

    def compact(cells):
        if wide == per:
            return cells.reshape(slots, 128)
        return jnp.concatenate([cells[s, 0:per, :] for s in range(n)], axis=0)

    mask = compact(mask3)
    halfmask[...] = mask.astype(BF16)

    loads[0].wait()
    loads[1].wait()

    used = vd.shape[0]
    sizes = [min(16, used - a * 16) for a in range(cols // 16)]

    def gather(a):
        size = sizes[a]
        return jnp.concatenate([
            vd[a * 16:a * 16 + size, r * 16:(r + 1) * 16, :].reshape(size * 16, 128)
            for r in range(slots // 16)], axis=1)

    alike = (iota((256, 256), 0) & 15) == (iota((256, 256), 1) & 15)

    def gram_rows(a):
        size = sizes[a]
        for r in range(slots // 16):
            rows16 = slice(r * 16, (r + 1) * 16)
            block = vd[a * 16:a * 16 + size, rows16, :] * halfmask[rows16, :][None]
            masked[a % 2, 0:size * 16, r * 128:(r + 1) * 128] = block.reshape(size * 16, 128)
        for b in range(a, cols // 16):
            high, wide_b = size * 16, sizes[b] * 16
            prod = dot(masked[a % 2, 0:high, :], gather(b), ((1,), (1,)))
            kept = jnp.where(alike[0:high, 0:wide_b], prod, 0.0).reshape(size, 16, wide_b)
            kept = jnp.sum(kept, axis=1)
            kbuf[a * 16:a * 16 + size, b * 256:b * 256 + wide_b] = 0.5 * kept if a == b else kept

    gram_rows(0)

    wait(pbuf, recv_sem.at[1])
    if wide == per:
        small[5].wait()
    returned = pbuf[...].reshape(total, 128)
    hi, mid, low = split3(returned)
    pext[EDGE:EDGE + lines, :] = dot(chooser, hi) + dot(chooser, mid) + dot(chooser, low)
    press_halo = halos(pext, 2, ())

    gram_rows(1)

    for move in field_halo:
        move.wait()
    for move in press_halo:
        move.wait()
    w, v, stiff, force = ext[0], ext[1], ext[2], pext[...]
    rows = lines + 2 * EDGE
    lane = iota((rows, 128), 1)
    for _ in range(SUBSTEPS):
        upper = pltpu.roll(w, 1, 0)
        beneath = pltpu.roll(w, rows - 1, 0)
        lft = jnp.where(lane == 0, 0.0, pltpu.roll(w, 1, 1))
        rgt = jnp.where(lane == 127, 0.0, pltpu.roll(w, 127, 1))
        lapl = upper + beneath + (lft + rgt) - 4.0 * w
        v = v + (stiff * lapl + force - DAMPING * v)
        w = w + v
    field = w[EDGE:EDGE + lines, :]
    hi, mid, low = split3(field)
    placed = dot(placer, hi) + dot(placer, mid) + dot(placer, low)
    obuf[...] = placed.reshape(n, wide, 128)
    peers(lambda p: send(obuf.at[p], xbuf.at[me], 4, p))
    xbuf[me] = obuf[me]
    field_ref[...] = field
    speed_ref[...] = v[EDGE:EDGE + lines, :]

    for a in range(2, cols // 16):
        gram_rows(a)
    spread = jnp.where((iota((cols * 16, 128), 0) >> 4) == iota((cols * 16, 128), 1), 1.0, 0.0)
    spread = spread.astype(BF16)
    hi, mid, low = split3(kbuf[...])
    value = dot(hi, spread) + dot(mid, spread) + dot(low, spread)
    gram[0:cols // 8] = value.reshape(cols // 8, 8, 128)
    peers(lambda p: send(gram.at[p], rsbuf.at[me], 2, p))
    rsbuf[me] = gram[me]

    wait(xbuf, recv_sem.at[4])
    small[4].wait()
    x_tilde = compact(xbuf[...])
    resid = (mask * (x_tilde - iter_v[...])).astype(BF16).astype(F32)

    def product(k, carry):
        for u in range(10):
            prow[pl.ds(k * 10 + u, 1), :] = jnp.sum(
                vd[k * 10 + u].astype(F32) * resid, axis=0, keepdims=True)
        return carry

    steps = (nc + npast) // 10
    lax.fori_loop(0, steps // 2, product, 0)

    wait(rsbuf, recv_sem.at[2])
    agbuf[me] = jnp.sum(rsbuf[...], axis=0)
    peers(lambda p: send(agbuf.at[me], agbuf.at[me], 3, p))

    lax.fori_loop(steps // 2, steps, product, 0)
    ones = jnp.ones((8, 128), BF16)
    hi, mid, low = split3(prow[...])
    arbuf[me] = (dot(ones, hi, ((1,), (1,))) + dot(ones, mid, ((1,), (1,)))
                 + dot(ones, low, ((1,), (1,))))
    peers(lambda p: send(arbuf.at[me], arbuf.at[me], 5, p))

    wait(agbuf, recv_sem.at[3])
    half = agbuf[0:16].reshape(128, 128)
    full = half + half.T
    lane2, sub2 = iota((nc, 128), 1), iota((nc, 128), 0)
    unit = jnp.where(lane2 == sub2 + 64, 1.0, 0.0)
    cross = full[nc:2 * nc, :]
    past_part = jnp.where(lane2 < nc, pltpu.roll(cross, 128 - nc, 1), 0.0)
    elim[0] = jnp.where(lane2 < nc, full[0:nc, :], 0.0) + unit
    elim[1] = past_part + unit + jnp.where((lane2 == sub2) & (sub2 >= npast), 1.0, 0.0)
    lane3, sub3 = iota((2, nc, 128), 2), iota((2, nc, 128), 1)

    lane1 = iota((2, 1, 128), 2)

    width = next(g for g in (4, 2, 1) if nc % g == 0)

    def lane_of(cells, lanes, j):
        return jnp.sum(jnp.where(lanes == j, cells, 0.0), axis=2, keepdims=True)

    def eliminate(i, carry):
        j = width * i
        now = elim[...]
        rows = [elim[:, pl.ds(j + u, 1), :] for u in range(width)]
        columns = [lane_of(now, lane3, j + u) for u in range(width)]
        entry = [[lane_of(rows[u], lane1, j + m) for m in range(u + 1)] for u in range(width)]
        for m in range(width):
            for u in range(m + 1, width):
                factor = entry[u][m] / entry[m][m]
                rows[u] = rows[u] - factor * rows[m]
                columns[u] = columns[u] - factor * columns[m]
                for k in range(m + 1, u + 1):
                    entry[u][k] = entry[u][k] - factor * entry[k][m]
        later = now
        for u in range(width):
            later = later - columns[u] * (rows[u] / entry[u][u])
        result = jnp.where(sub3 >= j + width, later, now)
        for u in range(1, width):
            result = jnp.where(sub3 == j + u, rows[u], result)
        elim[...] = result
        return carry

    lax.fori_loop(0, nc // width, eliminate, 0)
    done = elim[...]
    diag2 = lane2 == sub2
    inverse, pivots = [], []
    for part in range(2):
        inverse.append(jnp.where(lane2 < nc, pltpu.roll(done[part], 64, 1), 0.0))
        pivots.append(jnp.sum(jnp.where(diag2, done[part], 0.0), axis=1, keepdims=True))

    loads[2].wait()
    loads[3].wait()
    wait(arbuf, recv_sem.at[5])
    rhs = jnp.sum(arbuf[...], axis=0)

    def solve(part, vector):
        inner = jnp.sum(inverse[part] * vector, axis=1, keepdims=True) / pivots[part]
        return jnp.sum(inverse[part] * inner, axis=0, keepdims=True)

    coeff = -solve(0, rhs[0:1, :])
    carried = jnp.sum(cross * coeff, axis=1, keepdims=True)
    carried = jnp.sum(jnp.where(diag2, carried, 0.0), axis=0, keepdims=True)
    past = solve(1, pltpu.roll(rhs, 128 - nc, 1)[0:1, :] + carried)
    for part, vector in enumerate((coeff, -past)):
        column = jnp.sum(jnp.where(diag2, vector, 0.0), axis=1, keepdims=True)
        coefs[part * nc:(part + 1) * nc, :] = jnp.broadcast_to(
            column, (nc, 128)).astype(BF16).astype(F32)

    def accumulate(k, acc):
        for u in range(10):
            acc = acc + coefs[pl.ds(k * 10 + u, 1), :] * vs[k * 10 + u].astype(F32)
        return acc

    update = lax.fori_loop(0, (nc + npast) // 10, accumulate, jnp.zeros((slots, 128), F32))
    new_ref[...] = mask * (x_tilde + update)

    for phase, buf in enumerate((cnt, pbuf, rsbuf, agbuf, xbuf, arbuf)):
        wait(buf, send_sem.at[phase])


def hand_over(a, b, c, a_out, b_out, c_out, a_held, b_held, c_held, sems):
    pairs = ((a, a_held, a_out), (b, b_held, b_out), (c, c_held, c_out))
    fetch = [pltpu.make_async_copy(src, held, sems.at[0, i]) for i, (src, held, _) in enumerate(pairs)]
    store = [pltpu.make_async_copy(held, dst, sems.at[1, i]) for i, (_, held, dst) in enumerate(pairs)]
    for move in fetch:
        move.start()
    for move, after in zip(fetch, store):
        move.wait()
        after.start()
    for move in store:
        move.wait()


def local(press, iterate, displace, velocity, stiffness, owners, diff_cur, step_cur, diff_past, step_past):
    n = lax.axis_size("tile")
    lines, slots = displace.shape[0], iterate.shape[0]
    per = slots // n
    wide = max(8, per)
    nc, npast = diff_cur.shape[0], diff_past.shape[0]
    cols = -(-2 * nc // 16) * 16
    vmem = pl.BlockSpec(memory_space=pltpu.VMEM)
    hbm = pl.BlockSpec(memory_space=pl.ANY)
    tiles = pltpu.VMEM((n, 8, 128), F32)
    blocks = pltpu.VMEM((n, wide, 128), F32)
    outs = pl.pallas_call(
        functools.partial(kernel, n, per, wide),
        out_shape=(
            jax.ShapeDtypeStruct((slots, 128), F32),
            jax.ShapeDtypeStruct((lines, 128), F32),
            jax.ShapeDtypeStruct((lines, 128), F32),
        ),
        in_specs=[hbm] * 10,
        out_specs=(vmem, vmem, vmem),
        scratch_shapes=[
            pltpu.VMEM((-(-(nc + npast) // 8) * 8, slots, 128), BF16),
            pltpu.VMEM((nc + npast, slots, 128), BF16),
            pltpu.VMEM((2, 256, slots // 16 * 128), BF16),
            pltpu.VMEM((cols, cols * 16), F32),
            pltpu.VMEM((slots, 128), BF16),
            pltpu.VMEM((slots, 128), F32),
            pltpu.VMEM((1, lines), jnp.int32),
            pltpu.VMEM((3, lines + 2 * EDGE, 128), F32),
            pltpu.VMEM((lines + 2 * EDGE, 128), F32),
            tiles,
            pltpu.VMEM((slots if wide != per else 8, 128), F32),
            blocks if wide != per else pltpu.VMEM((8, 128), F32),
            blocks, blocks, blocks,
            tiles, tiles, tiles,
            pltpu.VMEM((128, 128), F32),
            tiles,
            pltpu.VMEM((2, nc, 128), F32),
            pltpu.VMEM((2 * nc, 128), F32),
            pltpu.SemaphoreType.DMA((4,)),
            pltpu.SemaphoreType.DMA((6,)),
            pltpu.SemaphoreType.DMA((6,)),
            pltpu.SemaphoreType.DMA((6,)),
            pltpu.SemaphoreType.DMA((4,)),
            pltpu.SemaphoreType.DMA((4,)),
        ],
        compiler_params=pltpu.CompilerParams(
            collective_id=0, has_side_effects=True, vmem_limit_bytes=62 * 1024 * 1024),
    )(press, iterate, displace, velocity, stiffness, owners.reshape(1, lines),
      diff_cur, step_cur, diff_past, step_past)
    return pl.pallas_call(
        hand_over,
        out_shape=tuple(jax.ShapeDtypeStruct(out.shape, out.dtype) for out in outs),
        in_specs=[hbm] * 3,
        out_specs=(hbm,) * 3,
        scratch_shapes=[pltpu.VMEM(out.shape, out.dtype) for out in outs]
        + [pltpu.SemaphoreType.DMA((2, 3))],
        compiler_params=pltpu.CompilerParams(vmem_limit_bytes=62 * 1024 * 1024),
    )(*outs)


def solution(mesh):
    rows = P(("runs", "tile"), None)
    deep = P(None, ("runs", "tile"), None)
    return jax.shard_map(
        local,
        mesh=mesh,
        in_specs=(rows,) * 6 + (deep,) * 4,
        out_specs=(rows, rows, rows),
        check_vma=False,
    )
```
